256 devices in a mesh: owner: 16 (over y_lo, z), blk: 16 (over y_hi, x, core).
Axes of the slice: x: 4, y: 4 (y_hi: 2, y_lo: 2; y = y_hi * 2 + y_lo), z: 8, core: 2. Of those that a mesh axis runs over, the one named last changes fastest.
Arguments:
- rhs_pivot: bfloat16 [16, 8192, 2048], P(None, 'owner', 'blk'), may hold values from -6 to 6
- block_pattern: int32 [16, 16, 16], P(None, 'owner', 'blk'), may hold values 0 or 1
- diag_inverse: bfloat16 [16, 8192, 512], P('blk', 'owner'), may hold values from -0.25 to 0.25
- right_factor: bfloat16 [16, 8192, 1024], P('blk', 'owner'), may hold values from -0.25 to 0.25
- left_factor: bfloat16 [16, 8192, 1024], P('blk', 'owner'), may hold values from -0.1875 to 0.1875
- tile_ranks: int32 [16, 16, 16], P('blk'), may hold values from 9 to 64
- contrib_rhs: bfloat16 [16, 8192, 2048], P('blk', 'owner'), may hold values from -6 to 6
- parent_map: int32 [16, 8192], replicated, may hold values from 0 to 8191, as said below
Outputs:
- pivot_solution: bfloat16 [16, 8192, 2048], P('blk', 'owner')
- parent_update: float32 [8192, 2048], P('owner', 'blk')
The draws below stay inside these ranges and needn't reach their ends.
Inputs may be any that keep to these rules, and one draw needn't show every extreme that they name: Each front's row of parent_map names every parent row exactly once; of the 512 rows of one contribution tile at most 64 go to any one parent tile of 512 rows, and in every front some tile sends exactly 64 rows to some parent tile.
All inputs are finite; a program needn't handle non-finite values. No bound on the sum of `block_pattern` on one device may be relied on, other than what follows from the above.
Results may differ from the reference program's by a relative error of at most 0.0022.
Values may be sent and summed in bfloat16 or wider, within the bound.
No kernel may reach another device: no remote copies, remote signals or barrier semaphores. Data moves between devices by JAX's collectives and lax.ppermute only.
A program may use at most 192 MiB of HBM per device.

```python
import jax
import jax.numpy as jnp
from jax import lax

TS = 512
RK = 64
R = 2048
CW = 128
NFR = 16
PT = 16
CT = 16
PTR = 8192
CBR = 8192
NCOL = 16


def front_map(key):
    average = TS // CT
    first_key, shift_key, inner_key, rows_key = jax.random.split(key, 4)
    order = jax.random.permutation(first_key, CT).astype(jnp.int32)
    shift = jax.random.randint(shift_key, (), 1, CT).astype(jnp.int32)
    tiles = jnp.arange(CT, dtype=jnp.int32)
    first = (order[:, None] == tiles[None, :]).astype(jnp.int32)
    second = (order[(tiles + shift) % CT][:, None] == tiles[None, :]).astype(jnp.int32)
    counts = average * (1 + first - second)
    row_end = jnp.cumsum(counts, axis=1)
    row_start = row_end - counts
    col_start = jnp.cumsum(counts, axis=0) - counts
    slots = jnp.arange(TS, dtype=jnp.int32)
    target_tile = jnp.sum((slots[None, :, None] >= row_end[:, None, :]).astype(jnp.int32), axis=2)
    offset = jnp.take_along_axis(col_start - row_start, target_tile, axis=1)
    local = offset + slots[None, :]
    inner = jax.random.permutation(inner_key, TS).astype(jnp.int32)
    values = target_tile * TS + inner[local]
    row_keys = jax.random.split(rows_key, CT)
    shuffles = jax.vmap(lambda k: jax.random.permutation(k, TS))(row_keys).astype(jnp.int32)
    values = jnp.take_along_axis(values, shuffles, axis=1)
    return values.reshape(CBR).astype(jnp.int32)


def draw_parent_map(key, part):
    key = jax.random.fold_in(key, 11)
    front_keys = jax.random.split(key, NFR)
    return jax.vmap(front_map)(front_keys)


def with_ends(drawn, rng, low, top_value):
    longest = drawn.shape.index(max(drawn.shape))
    spots = []
    for shift in (0, 1):
        where = [jax.random.randint(jax.random.fold_in(rng, axis), (), 0, length) for axis, length in enumerate(drawn.shape)]
        where[longest] = (where[longest] + shift) % drawn.shape[longest]
        spots.append(tuple(where))
    return drawn.at[spots[0]].set(low).at[spots[1]].set(top_value)


def block_levels(key, dims, cuts, smallest, top_value):
    gain = 1.0
    for dim, shards_of in cuts:
        draws = jax.random.uniform(jax.random.fold_in(jax.random.fold_in(key, 6), dim), (shards_of,), jnp.float32, smallest / len(cuts), top_value / len(cuts))
        gain = gain * jnp.repeat(jnp.exp(draws), dims[dim] // shards_of).reshape((-1,) + (1,) * (len(dims) - 1 - dim))
    return gain


def gaussian(rng, dims, deviation, reach, cuts=(), held_as=jnp.bfloat16):
    values = jax.random.normal(rng, dims, jnp.float32) * deviation
    if len(cuts) > 0:
        values = block_levels(rng, dims, cuts, -0.22, 0.18) * values
    return jnp.clip(values, min=-reach, max=reach).astype(held_as)


def setup_inputs(seed: int = 0) -> dict:
    key_of = jax.random.split(jax.random.key(seed), 9)
    return {
        "rhs_pivot": gaussian(key_of[0], (NFR, PTR, R), 1.0, 6.0, ((1, 16), (2, 16))),
        "block_pattern": with_ends((jax.random.randint(key_of[1], (NFR, PT, NCOL), 0, 3) < 2).astype(jnp.int32), jax.random.fold_in(key_of[1], 1), 0, 1),
        "diag_inverse": gaussian(key_of[2], (NFR, PTR, TS), TS ** -0.5, 0.25, ((0, 16), (1, 16))),
        "right_factor": gaussian(key_of[3], (NFR, PTR, CT * RK), TS ** -0.5, 0.25, ((0, 16), (1, 16))),
        "left_factor": gaussian(key_of[4], (NFR, CBR, PT * RK), (PT * RK) ** -0.5, 0.1875, ((0, 16), (1, 16))),
        "tile_ranks": with_ends(jax.random.randint(key_of[5], (NFR, CT, PT), RK // 8 + 1, RK + 1), jax.random.fold_in(key_of[5], 1), RK // 8 + 1, RK).astype(jnp.int32),
        "contrib_rhs": gaussian(key_of[6], (NFR, CBR, R), 1.0, 6.0, ((0, 16), (1, 16))),
        "parent_map": draw_parent_map(jax.random.fold_in(key_of[8], 71), 0),
    }


def one_front(items):
    rhs_f, pattern_f, inverse_f, right_f, left_f, ranks_f, contrib_f = items
    expand = jnp.repeat(pattern_f, CW, axis=1).astype(jnp.bfloat16)
    masked = rhs_f.reshape(PT, TS, R) * expand[:, None, :]
    inverse_tiles = inverse_f.reshape(PT, TS, TS).astype(jnp.float32)
    solved = jnp.einsum('jst,jtc->jsc', inverse_tiles, masked.astype(jnp.float32)).astype(jnp.bfloat16)
    right_tiles = right_f.reshape(PT, TS, CT * RK).astype(jnp.float32)
    projected = jnp.einsum('jtq,jtc->jqc', right_tiles, solved.astype(jnp.float32))
    projected = projected.reshape(PT, CT, RK, R)
    rank_mask = jnp.arange(RK, dtype=jnp.int32)[None, None, :] < jnp.transpose(ranks_f)[:, :, None]
    projected = jnp.where(rank_mask[..., None], projected, 0.0).astype(jnp.bfloat16)
    by_row = jnp.transpose(projected, (1, 0, 2, 3)).reshape(CT, PT * RK, R).astype(jnp.float32)
    left_tiles = left_f.reshape(CT, TS, PT * RK).astype(jnp.float32)
    product = jnp.einsum('itq,iqc->itc', left_tiles, by_row).reshape(CBR, R)
    reduced = contrib_f.astype(jnp.float32) - product
    return solved.reshape(PTR, R), reduced


def reference(rhs_pivot, block_pattern, diag_inverse, right_factor, left_factor, tile_ranks, contrib_rhs, parent_map):
    solved, reduced = lax.map(one_front, (rhs_pivot, block_pattern, diag_inverse, right_factor, left_factor, tile_ranks, contrib_rhs))

    def accumulate(total, items):
        rows_f, map_f = items
        return total.at[map_f].add(rows_f.astype(jnp.float32)), None

    start_total = jnp.zeros((CBR, R), jnp.float32)
    parent_update, unused = lax.scan(accumulate, start_total, (reduced, parent_map))
    return solved, parent_update
```

```python
import functools

import jax
import jax.numpy as jnp
from jax import lax
from jax.experimental import pallas as pl
from jax.experimental.pallas import tpu as pltpu
from jax.sharding import PartitionSpec as P

RK = 64
CW = 128
WIN = 80
EXP_ROWS = 16
CODE_BITS = 14
VMEM_LIMIT = 48 * 1024 * 1024


def vmem():
    return pl.BlockSpec(memory_space=pltpu.VMEM)


def smem():
    return pl.BlockSpec(memory_space=pltpu.SMEM)


def params():
    return pltpu.CompilerParams(vmem_limit_bytes=VMEM_LIMIT)


def cost(flops, bytes_accessed):
    return pl.CostEstimate(flops=int(flops), bytes_accessed=int(bytes_accessed), transcendentals=0)


def groups_of(count):
    if count == 16:
        return [[0, 1, 2, 3], [4, 5, 8, 9, 12, 13, 10, 11], [14, 15, 6, 7]]
    order = list(range(count))
    return [order[: count // 4], order[count // 4 : 3 * count // 4], order[3 * count // 4 :]]


def mask_body(count, fronts_ref, pattern_ref, *refs):
    for step in range(count):
        keep = pattern_ref[fronts_ref[step]].astype(jnp.float32)
        source, target = refs[step], refs[count + step]
        target[...] = (source[0].astype(jnp.float32) * keep).astype(jnp.bfloat16)


def mask_fronts(rhs, pattern, fronts):
    count = fronts.shape[0]
    rows, cols = rhs.shape[1:]

    def pick(step):
        return lambda i, fronts_ref, pattern_ref: (fronts_ref[step], 0, 0)

    return pl.pallas_call(
        functools.partial(mask_body, count),
        out_shape=[jax.ShapeDtypeStruct((rows, cols), jnp.bfloat16)] * count,
        grid_spec=pltpu.PrefetchScalarGridSpec(
            num_scalar_prefetch=2,
            grid=(1,),
            in_specs=[pl.BlockSpec((1, rows, cols), pick(step)) for step in range(count)],
            out_specs=[pl.BlockSpec((rows, cols), lambda i, a, b: (0, 0))] * count,
        ),
        compiler_params=params(),
        cost_estimate=cost(count * rows * cols, 4 * count * rows * cols),
        name="mask_fronts",
    )(fronts, pattern, *([rhs] * count))


def right_body(right_ref, keep_ref, out_ref):
    kept = right_ref[...].astype(jnp.float32) * keep_ref[...]
    out_ref[...] = kept.T.astype(jnp.bfloat16)


def right_transposed(right, keep):
    rows, width = right.shape
    return pl.pallas_call(
        right_body,
        out_shape=jax.ShapeDtypeStruct((width, rows), jnp.bfloat16),
        in_specs=[vmem()] * 2,
        out_specs=vmem(),
        compiler_params=params(),
        cost_estimate=cost(rows * width, 4 * rows * width),
        name="right_transposed",
    )(right, keep)


def solve_body(count, inverse_ref, right_ref, *refs):
    sources = refs[:count]
    solved_ref, projected_ref = refs[count:]
    tiles = projected_ref.shape[0]
    for start in range(0, count, 2):
        width = min(2, count - start) * CW
        block = jnp.concatenate([ref[...] for ref in sources[start : start + 2]], axis=1)
        solved = jnp.dot(inverse_ref[...], block, preferred_element_type=jnp.float32)
        solved = solved.astype(jnp.bfloat16)
        for step in range(width // CW):
            solved_ref[start + step] = solved[:, step * CW : (step + 1) * CW]
        projected = jnp.dot(right_ref[...], solved, preferred_element_type=jnp.float32)
        projected_ref[:, :, start * CW : start * CW + width] = projected.astype(
            jnp.bfloat16
        ).reshape(tiles, RK, width)


def solve_group(inverse, right, blocks):
    count = len(blocks)
    rows = inverse.shape[0]
    width = right.shape[0]
    return pl.pallas_call(
        functools.partial(solve_body, count),
        out_shape=[
            jax.ShapeDtypeStruct((count, rows, CW), jnp.bfloat16),
            jax.ShapeDtypeStruct((width // RK, RK, count * CW), jnp.bfloat16),
        ],
        in_specs=[vmem()] * (2 + count),
        out_specs=[vmem()] * 2,
        compiler_params=params(),
        cost_estimate=cost(2 * rows * (rows + width) * count * CW, 2 * count * CW * (2 * rows + width)),
        name="solve_group",
    )(inverse, right, *blocks)


def place_body(starts, columns_ref, *refs):
    out_ref = refs[-1]
    step = pl.program_id(0)
    for begin, end, ref in zip(starts[:-1], starts[1:], refs[:-1]):

        @pl.when((step >= begin) & (step < end))
        def _(ref=ref):
            out_ref[0] = ref[0]


def place_blocks(columns, parts):
    starts = [0]
    for part in parts:
        starts.append(starts[-1] + part.shape[0])
    rows = parts[0].shape[1]

    def pick(begin, end):
        return lambda i, columns_ref: (jnp.clip(i - begin, 0, end - begin - 1), 0, 0)

    return pl.pallas_call(
        functools.partial(place_body, starts),
        out_shape=jax.ShapeDtypeStruct((1, rows, starts[-1] * CW), jnp.bfloat16),
        grid_spec=pltpu.PrefetchScalarGridSpec(
            num_scalar_prefetch=1,
            grid=(starts[-1],),
            in_specs=[
                pl.BlockSpec((1, rows, CW), pick(begin, end))
                for begin, end in zip(starts[:-1], starts[1:])
            ],
            out_specs=pl.BlockSpec((1, rows, CW), lambda i, columns_ref: (0, 0, columns_ref[i])),
        ),
        compiler_params=params(),
        cost_estimate=cost(0, 4 * rows * starts[-1] * CW),
        name="place_blocks",
    )(columns, *parts)


def order_row(row_keys, column_keys):
    smaller = (column_keys < row_keys).astype(jnp.float32)
    return jnp.sum(smaller, axis=0, keepdims=True)


def sort_body(columns_ref, row_ref, column_ref, left_ref, contrib_ref, left_out, contrib_out, one_hot):
    rows = row_ref.shape[1]

    @pl.when(pl.program_id(0) == 0)
    def _():
        rank = order_row(row_ref[...], column_ref[...])
        place = lax.broadcasted_iota(jnp.int32, (rows, rows), 0).astype(jnp.float32)
        one_hot[...] = (place == rank).astype(jnp.float32).astype(jnp.bfloat16)
        left = jnp.dot(one_hot[...], left_ref[...], preferred_element_type=jnp.float32)
        left_out[...] = left.astype(jnp.bfloat16)

    sorted_rows = jnp.dot(one_hot[...], contrib_ref[...], preferred_element_type=jnp.float32)
    contrib_out[0] = sorted_rows.astype(jnp.bfloat16)


def sort_rows(columns, keys, left, contrib):
    rows, width = left.shape
    count = columns.shape[0]
    return pl.pallas_call(
        sort_body,
        out_shape=[
            jax.ShapeDtypeStruct((rows, width), jnp.bfloat16),
            jax.ShapeDtypeStruct((count, rows, CW), jnp.bfloat16),
        ],
        grid_spec=pltpu.PrefetchScalarGridSpec(
            num_scalar_prefetch=1,
            grid=(count,),
            in_specs=[
                pl.BlockSpec((1, rows), lambda i, c: (0, 0)),
                pl.BlockSpec((rows, 1), lambda i, c: (0, 0)),
                pl.BlockSpec((rows, width), lambda i, c: (0, 0)),
                pl.BlockSpec((rows, CW), lambda i, c: (0, c[i])),
            ],
            out_specs=[
                pl.BlockSpec((rows, width), lambda i, c: (0, 0)),
                pl.BlockSpec((1, rows, CW), lambda i, c: (i, 0, 0)),
            ],
            scratch_shapes=[pltpu.VMEM((rows, rows), jnp.bfloat16)],
        ),
        compiler_params=params(),
        cost_estimate=cost(2 * rows * rows * (width + count * CW), 4 * rows * (width + count * CW)),
        name="sort_rows",
    )(columns, keys.reshape(1, rows), keys.reshape(rows, 1), left, contrib)


def target_body(row_ref, column_ref, out_ref):
    rows = row_ref.shape[2]
    keys = row_ref[0]
    rank = order_row(keys, column_ref[0])
    place = lax.broadcasted_iota(jnp.int32, (rows, rows), 0).astype(jnp.float32)
    ordered = jnp.sum(jnp.where(place == rank, keys, 0.0), axis=1, keepdims=True)
    out_ref[0] = jnp.broadcast_to(ordered, (rows, CW)).astype(jnp.int32)


def sorted_targets(maps):
    count, rows = maps.shape
    keys = maps.astype(jnp.float32)
    return pl.pallas_call(
        target_body,
        out_shape=jax.ShapeDtypeStruct((count, rows, CW), jnp.int32),
        grid=(count,),
        in_specs=[
            pl.BlockSpec((1, 1, rows), lambda i: (i, 0, 0)),
            pl.BlockSpec((1, rows, 1), lambda i: (i, 0, 0)),
        ],
        out_specs=pl.BlockSpec((1, rows, CW), lambda i: (i, 0, 0)),
        compiler_params=params(),
        cost_estimate=cost(5 * count * rows * rows, 4 * count * rows * CW),
        name="sorted_targets",
    )(keys.reshape(count, 1, rows), keys.reshape(count, rows, 1))


def update_body(count, first, left_ref, projected_ref, contrib_ref, *out_refs):
    rows, width = left_ref.shape
    for start in range(0, count, 2):
        span = min(2, count - start)
        part = projected_ref[:, :, start * CW : (start + span) * CW].reshape(width, span * CW)
        product = jnp.dot(left_ref[...], part, preferred_element_type=jnp.float32)
        for step in range(span):
            reduced = contrib_ref[first + start + step].astype(jnp.float32)
            reduced = reduced - product[:, step * CW : (step + 1) * CW]
            top = jnp.max(jnp.abs(reduced), axis=0, keepdims=True)
            exponent = jnp.floor(jnp.log2(jnp.maximum(top, 2.0**-108))) + 1.0
            scale = jnp.exp2(CODE_BITS - exponent)
            code = jnp.floor(reduced * scale + 0.5).astype(jnp.int32)
            out = out_refs[start + step]
            out[:rows, :] = code.astype(jnp.int16)
            out[rows:, :] = jnp.broadcast_to(exponent.astype(jnp.int32), (EXP_ROWS, CW)).astype(jnp.int16)


def update_group(left, projected, contrib, first):
    rows, width = left.shape
    count = projected.shape[2] // CW
    return pl.pallas_call(
        functools.partial(update_body, count, first),
        out_shape=[jax.ShapeDtypeStruct((rows + EXP_ROWS, CW), jnp.int16)] * count,
        in_specs=[vmem()] * 3,
        out_specs=[vmem()] * count,
        compiler_params=params(),
        cost_estimate=cost(2 * rows * width * count * CW, 2 * count * CW * (width + 2 * rows)),
        name="update_group",
    )(left, projected, contrib)


def scatter_body(count, first, has_partial, starts_ref, targets_ref, *refs):
    sources = refs[:count]
    partial_ref = refs[count] if has_partial else None
    out_ref, values, one_hot = refs[-3:]
    rows = targets_ref.shape[1]
    tile = pl.program_id(0)

    @pl.when(tile == 0)
    def _():
        for step in range(count):
            code = sources[step][:rows, :].astype(jnp.int32).astype(jnp.float32)
            exponent = sources[step][rows:, :].astype(jnp.int32).astype(jnp.float32)[:1]
            value = code * jnp.exp2(exponent - CODE_BITS)
            high = value.astype(jnp.bfloat16)
            low = (value - high.astype(jnp.float32)).astype(jnp.bfloat16)
            values[step * rows : (step + 1) * rows, :CW] = high
            values[step * rows : (step + 1) * rows, CW:] = low

    parts = []
    lane = lax.broadcasted_iota(jnp.int32, (WIN, rows), 1) + tile * rows
    for step in range(count):
        begin = jnp.minimum((starts_ref[first + step, tile] // 16) * 16, rows - WIN)
        begin = pl.multiple_of(begin, 16)
        target = targets_ref[first + step, pl.ds(begin, WIN), :]
        target = jnp.concatenate([target] * (rows // CW), axis=1)
        match = jnp.where(target == lane, 1.0, 0.0)
        one_hot[step * WIN : (step + 1) * WIN, :] = match.astype(jnp.bfloat16)
        parts.append(values[pl.ds(pl.multiple_of(step * rows + begin, 16), WIN), :])
    window = jnp.concatenate(parts, axis=0)
    total = lax.dot_general(
        window, one_hot[...], (((0,), (0,)), ((), ())), preferred_element_type=jnp.float32
    )
    total = total[:CW] + total[CW:]
    if has_partial:
        total = total + partial_ref[0]
    out_ref[0] = total.astype(out_ref.dtype)


def scatter_rows(starts, targets, first, coded, partial, out_dtype):
    count = len(coded)
    rows = targets.shape[1]
    tiles = starts.shape[1]
    has_partial = partial is not None
    tile_spec = pl.BlockSpec((1, CW, rows), lambda t: (t, 0, 0))
    whole = pl.BlockSpec((rows + EXP_ROWS, CW), lambda t: (0, 0))
    extra = [tile_spec] if has_partial else []
    operands = [partial] if has_partial else []
    return pl.pallas_call(
        functools.partial(scatter_body, count, first, has_partial),
        out_shape=jax.ShapeDtypeStruct((tiles, CW, rows), out_dtype),
        grid=(tiles,),
        in_specs=[smem(), pl.BlockSpec(targets.shape, lambda t: (0, 0, 0))] + [whole] * count + extra,
        out_specs=tile_spec,
        scratch_shapes=[
            pltpu.VMEM((count * rows, 2 * CW), jnp.bfloat16),
            pltpu.VMEM((count * WIN, rows), jnp.bfloat16),
        ],
        compiler_params=params(),
        cost_estimate=cost(4 * CW * count * WIN * rows * tiles, 8 * tiles * CW * rows),
        name="scatter_rows",
    )(starts, targets, *coded, *operands)


def total_body(parts_ref, out_ref):
    total = jnp.sum(parts_ref[...].astype(jnp.float32), axis=0)
    out_ref[...] = total.T


def total_rows(parts):
    tiles, cols, rows = parts.shape
    return pl.pallas_call(
        total_body,
        out_shape=jax.ShapeDtypeStruct((rows, cols), jnp.float32),
        grid=(rows // CW,),
        in_specs=[pl.BlockSpec((tiles, cols, CW), lambda i: (0, 0, i))],
        out_specs=pl.BlockSpec((CW, cols), lambda i: (i, 0)),
        compiler_params=params(),
        cost_estimate=cost(tiles * cols * rows, 2 * tiles * cols * rows),
        name="total_rows",
    )(parts)


def after(first, *later):
    held = lax.optimization_barrier((first,) + later)
    return held[1:]


def per_device(
    rhs_pivot,
    block_pattern,
    diag_inverse,
    right_factor,
    left_factor,
    tile_ranks,
    contrib_rhs,
    parent_map,
):
    owner = lax.axis_index("owner")
    blk = lax.axis_index("blk")
    partners = lax.axis_size("blk")
    inverse, right = diag_inverse[0], right_factor[0]
    left, contrib = left_factor[0], contrib_rhs[0]
    rows = inverse.shape[0]
    tiles = lax.axis_size("owner")
    groups = groups_of(partners)
    order = sum(groups, [])
    firsts = [order.index(group[0]) for group in groups]
    columns = jnp.bitwise_xor(blk, jnp.array(order, jnp.int32))
    pattern = block_pattern.reshape(-1)

    def exchange(value, k):
        if k == 0:
            return value
        return lax.ppermute(value, "blk", [(i, i ^ k) for i in range(partners)])

    ranks_here = lax.dynamic_index_in_dim(tile_ranks[0], owner, 1, keepdims=False)
    keep = jnp.arange(RK, dtype=jnp.int32)[None, :] < ranks_here[:, None]
    keep = keep.astype(jnp.float32).reshape(1, -1)

    received = []
    for first, group in zip(firsts, groups):
        masked = mask_fronts(rhs_pivot, pattern, columns[first : first + len(group)])
        received.append([exchange(value, k) for value, k in zip(masked, group)])

    right_t = right_transposed(right, keep)

    solved, projected = [], []
    for blocks in received:
        part, sent = solve_group(inverse, right_t, blocks)
        solved.append(part)
        projected.append(lax.all_to_all(sent, "owner", split_axis=0, concat_axis=0, tiled=True))

    maps = lax.dynamic_slice_in_dim(parent_map, owner * rows, rows, 1)
    maps = jnp.take(maps, columns, axis=0)
    own_keys = lax.dynamic_slice_in_dim(
        lax.dynamic_index_in_dim(parent_map, blk, 0, keepdims=False), owner * rows, rows, 0
    ).astype(jnp.float32)
    edges = jnp.arange(tiles, dtype=jnp.int32) * rows
    starts = jnp.sum((maps[:, :, None] < edges[None, None, :]).astype(jnp.int32), axis=1)
    own_keys, maps = after(solved[0], own_keys, maps)
    left_sorted, contrib_sorted = sort_rows(columns, own_keys, left, contrib)
    targets = sorted_targets(maps)

    arrived = []
    for first, group, part in zip(firsts, groups, projected):
        coded = update_group(left_sorted, part, contrib_sorted, first)
        arrived.append([exchange(value, k) for value, k in zip(coded, group)])

    partial = scatter_rows(starts, targets, 0, arrived[0] + arrived[1], None, jnp.float32)
    parts = scatter_rows(starts, targets, firsts[2], arrived[2], partial, jnp.bfloat16)
    parts = lax.all_to_all(parts, "owner", split_axis=0, concat_axis=0, tiled=True)
    parent_update = total_rows(parts)
    pivot_solution = place_blocks(columns, solved)
    return (pivot_solution, parent_update)


def solution(mesh):
    return jax.shard_map(
        per_device,
        mesh=mesh,
        in_specs=(
            P(None, "owner", "blk"),
            P(None, "owner", "blk"),
            P("blk", "owner", None),
            P("blk", "owner", None),
            P("blk", "owner", None),
            P("blk", None, None),
            P("blk", "owner", None),
            P(),
        ),
        out_specs=(P("blk", "owner", None), P("owner", "blk")),
        check_vma=False,
    )
```

```python
import functools

import jax
import jax.numpy as jnp
from jax import lax
from jax.experimental import pallas as pl
from jax.experimental.pallas import tpu as pltpu
from jax.sharding import PartitionSpec as P

RK = 64
CW = 128
WIN = 144
HALF = CW // 2
EXP_ROWS = 16
RING = 8
TILE_BATCH = 4
CODE_BITS = 14
MIB = 1024 * 1024


def vmem():
    return pl.BlockSpec(memory_space=pltpu.VMEM)


def smem():
    return pl.BlockSpec(memory_space=pltpu.SMEM)


def token_shape():
    return jax.ShapeDtypeStruct((8, CW), jnp.float32)


def token_spec():
    return pl.BlockSpec((8, CW), lambda *grid: (0, 0))


def set_token(token_ref):
    token_ref[...] = jnp.zeros_like(token_ref)


def untouched(count):
    return [pl.BlockSpec(memory_space=pltpu.HBM)] * count


def params(mib):
    return pltpu.CompilerParams(vmem_limit_bytes=mib * MIB)


def cost(flops, bytes_accessed):
    return pl.CostEstimate(flops=int(flops), bytes_accessed=int(bytes_accessed), transcendentals=0)


def groups_of(count):
    if count == 8:
        return [[4, 5, 6, 2], [7, 3, 1, 0]]
    return [list(range(count // 2, count)), list(range(count // 2))]


def halves(first, second):
    left = jnp.concatenate([first[:, :HALF], second[:, :HALF]], axis=1)
    right = jnp.concatenate([first[:, HALF:], second[:, HALF:]], axis=1)
    return left, right


def swapped(flag, first, second):
    return jnp.where(flag, second, first), jnp.where(flag, first, second)


def mask_body(pattern_ref, rhs_ref, out_ref, token_ref):
    for step in range(rhs_ref.shape[0]):
        front = pl.program_id(0) * rhs_ref.shape[0] + step
        keep = pattern_ref[front].astype(jnp.float32)
        out_ref[step] = (rhs_ref[step].astype(jnp.float32) * keep).astype(jnp.bfloat16)
    set_token(token_ref)


def mask_all(rhs, pattern):
    count, rows, cols = rhs.shape
    spec = pl.BlockSpec((4, rows, cols), lambda i: (i, 0, 0))
    return pl.pallas_call(
        mask_body,
        out_shape=[pltpu.HBM(rhs.shape, jnp.bfloat16), token_shape()],
        grid=(count // 4,),
        in_specs=[smem(), spec],
        out_specs=[spec, token_spec()],
        compiler_params=params(60),
        cost_estimate=cost(count * rows * cols, 4 * count * rows * cols),
        name="mask_all",
    )(pattern, rhs)


def right_body(ring, odd_ref, right_ref, keep_ref, out_ref):
    kept = (right_ref[...].astype(jnp.float32) * keep_ref[...]).T
    span = ring * RK
    pieces = []
    for begin in range(0, kept.shape[0], span):
        pieces += [kept[begin + RK : begin + span], kept[begin : begin + RK]]
    turned = jnp.concatenate(pieces, axis=0)
    out_ref[...] = jnp.where(odd_ref[0] > 0, turned, kept).astype(jnp.bfloat16)


def right_transposed(odd, right, keep, ring):
    rows, width = right.shape
    return pl.pallas_call(
        functools.partial(right_body, ring),
        out_shape=pltpu.HBM((width, rows), jnp.bfloat16),
        in_specs=[smem()] + [vmem()] * 2,
        out_specs=vmem(),
        compiler_params=params(16),
        cost_estimate=cost(rows * width, 4 * rows * width),
        name="right_transposed",
    )(odd, right, keep)


def solve_body(count, ring, pairs_ref, odd_ref, inverse_ref, right_ref, *refs):
    sources = refs[:count]
    solved_ref, projected_ref, token_ref = refs[-3:]
    set_token(token_ref)
    depth = projected_ref.shape[0]
    odd = odd_ref[0]
    for step in range(count):
        block = jnp.concatenate(halves(sources[step][0], sources[step][1]), axis=1)
        solved = jnp.dot(inverse_ref[...], block, preferred_element_type=jnp.float32)
        solved = solved.astype(jnp.bfloat16)
        solved_ref[step, 0], solved_ref[step, 1] = halves(solved[:, :CW], solved[:, CW:])
        projected = jnp.dot(right_ref[...], solved, preferred_element_type=jnp.float32)
        projected = projected.astype(jnp.bfloat16)
        span = slice(step * CW, (step + 1) * CW)
        for begin in range(0, depth, ring):
            for tile in range(0, ring, 2):
                row = (begin + tile) * RK
                pair = projected[row : row + 2 * RK]
                projected_ref[begin + tile + 1, :, span] = pair[:, CW:]
                projected_ref[begin + lax.rem(tile + 2 * odd, ring), :, span] = pair[:, :CW]


def solve_group(pairs, odd, inverse, right, blocks, ring, earlier):
    count = pairs.shape[0]
    rows = inverse.shape[0]
    width = right.shape[0]
    depth = width // RK

    def whole(shape):
        return pl.BlockSpec(shape, lambda i, pairs_ref, odd_ref: (0,) * len(shape))

    def pick(step):
        return lambda i, pairs_ref, odd_ref: (pairs_ref[step], 0, 0)

    return pl.pallas_call(
        functools.partial(solve_body, count, ring),
        out_shape=[
            pltpu.HBM((count, 2, rows, CW), jnp.bfloat16),
            pltpu.HBM((depth, 2 * RK, count * CW), jnp.bfloat16),
            token_shape(),
        ],
        grid_spec=pltpu.PrefetchScalarGridSpec(
            num_scalar_prefetch=2,
            grid=(1,),
            in_specs=[whole((rows, rows)), whole((width, rows))]
            + [pl.BlockSpec((2, rows, CW), pick(step)) for step in range(count)]
            + untouched(len(earlier)),
            out_specs=[
                whole((count, 2, rows, CW)),
                whole((depth, 2 * RK, count * CW)),
                token_spec(),
            ],
        ),
        compiler_params=params(20),
        cost_estimate=cost(4 * rows * (rows + width) * count * CW, 4 * count * CW * (2 * rows + width)),
        name="solve_group",
    )(pairs, odd, inverse, right, *([blocks] * count), *earlier)


def place_body(starts, pairs_ref, *refs):
    out_ref = refs[-1]
    step = pl.program_id(0)
    for begin, end, ref in zip(starts[:-1], starts[1:], refs[:-1]):

        @pl.when((step >= begin) & (step < end))
        def _(ref=ref):
            out_ref[0, :, :CW] = ref[0, 0]
            out_ref[0, :, CW:] = ref[0, 1]


def place_blocks(pairs, parts):
    starts = [0]
    for part in parts:
        starts.append(starts[-1] + part.shape[0])
    rows = parts[0].shape[2]

    def pick(begin, end):
        return lambda i, pairs_ref: (jnp.clip(i - begin, 0, end - begin - 1), 0, 0, 0)

    return pl.pallas_call(
        functools.partial(place_body, starts),
        out_shape=jax.ShapeDtypeStruct((1, rows, starts[-1] * 2 * CW), jnp.bfloat16),
        grid_spec=pltpu.PrefetchScalarGridSpec(
            num_scalar_prefetch=1,
            grid=(starts[-1],),
            in_specs=[
                pl.BlockSpec((1, 2, rows, CW), pick(begin, end))
                for begin, end in zip(starts[:-1], starts[1:])
            ],
            out_specs=pl.BlockSpec((1, rows, 2 * CW), lambda i, pairs_ref: (0, 0, pairs_ref[i])),
        ),
        compiler_params=params(6),
        cost_estimate=cost(0, 8 * rows * starts[-1] * CW),
        name="place_blocks",
    )(pairs, *parts)


def pack_body(high_ref, contrib_ref, after_ref, keep_ref, send_ref):
    high = high_ref[0] > 0
    for step in range(keep_ref.shape[1] // CW):
        even = contrib_ref[:, 2 * step * CW : (2 * step + 1) * CW]
        other = contrib_ref[:, (2 * step + 1) * CW : (2 * step + 2) * CW]
        span = slice(step * CW, (step + 1) * CW)
        keep_ref[:, span], send_ref[:, span] = swapped(high, *halves(even, other))


def pack_contrib(high, contrib, earlier):
    rows, cols = contrib.shape
    spec = pl.BlockSpec((rows, cols // 4), lambda i: (0, i))
    return pl.pallas_call(
        pack_body,
        out_shape=[pltpu.HBM((rows, cols // 2), jnp.bfloat16)] * 2,
        grid=(2,),
        in_specs=[smem(), pl.BlockSpec((rows, cols // 2), lambda i: (0, i))] + untouched(1),
        out_specs=[spec] * 2,
        compiler_params=params(60),
        cost_estimate=cost(rows * cols, 4 * rows * cols),
        name="pack_contrib",
    )(high, contrib, earlier)


def ordering(keys):
    rows = keys.shape[1]
    column = jnp.broadcast_to(keys, (CW, rows)).T
    smaller = (jnp.concatenate([column] * (rows // CW), axis=1) < keys).astype(jnp.float32)
    rank = jnp.sum(smaller, axis=0, keepdims=True)
    place = lax.broadcasted_iota(jnp.int32, (rows, rows), 0).astype(jnp.float32)
    return jnp.where(place == rank, 1.0, 0.0).astype(jnp.bfloat16)


def sort_body(
    high_ref, keys_ref, own_ref, other_ref, kept_ref, got_ref, left_out, contrib_out, token_ref, one_hot
):
    rows = own_ref.shape[0]

    @pl.when(pl.program_id(0) == 0)
    def _():
        one_hot[...] = ordering(keys_ref[...])
        set_token(token_ref)

    def sort(value, begin):
        order = one_hot[:, begin : begin + rows]
        return jnp.dot(order, value, preferred_element_type=jnp.float32)

    own, other = sort(own_ref[...], 0), sort(other_ref[...], rows)
    low, top = swapped(high_ref[0] > 0, own, other)
    for step in range(low.shape[1] // CW):
        span = slice(step * CW, (step + 1) * CW)
        pair = halves(low[:, span], top[:, span])
        left_out[:, 2 * step * CW : (2 * step + 1) * CW] = pair[0].astype(jnp.bfloat16)
        left_out[:, (2 * step + 1) * CW : (2 * step + 2) * CW] = pair[1].astype(jnp.bfloat16)

    contrib = sort(kept_ref[...], 0) + sort(got_ref[...], rows)
    for step in range(contrib_out.shape[0]):
        contrib_out[step] = contrib[:, step * CW : (step + 1) * CW].astype(jnp.bfloat16)


def sort_rows(high, keys, own, other, kept, got):
    rows, width = own.shape
    cols = kept.shape[1]
    joint = 2 * rows
    steps = min(4, cols // CW)
    spread = min(steps, width // CW)
    return pl.pallas_call(
        sort_body,
        out_shape=[
            pltpu.HBM((joint, 2 * width), jnp.bfloat16),
            pltpu.HBM((cols // CW, joint, CW), jnp.bfloat16),
            token_shape(),
        ],
        grid=(steps,),
        in_specs=[
            smem(),
            pl.BlockSpec((1, joint), lambda i: (0, 0)),
            pl.BlockSpec((rows, width // spread), lambda i: (0, i % spread)),
            pl.BlockSpec((rows, width // spread), lambda i: (0, i % spread)),
            pl.BlockSpec((rows, cols // steps), lambda i: (0, i)),
            pl.BlockSpec((rows, cols // steps), lambda i: (0, i)),
        ],
        out_specs=[
            pl.BlockSpec((joint, 2 * width // spread), lambda i: (0, i % spread)),
            pl.BlockSpec((cols // CW // steps, joint, CW), lambda i: (i, 0, 0)),
            token_spec(),
        ],
        scratch_shapes=[pltpu.VMEM((joint, joint), jnp.bfloat16)],
        compiler_params=params(28),
        cost_estimate=cost(2 * joint * rows * (2 * width + 2 * cols), 8 * rows * (width + cols)),
        name="sort_rows",
    )(high, keys.reshape(1, joint), own, other, kept, got)


def target_body(keys_ref, after_ref, out_ref, token_ref):
    for step in range(keys_ref.shape[0]):
        keys = keys_ref[step]
        out_ref[step] = jnp.broadcast_to(keys, (CW, keys.shape[1])).T
    set_token(token_ref)


def sorted_targets(maps, earlier):
    count, rows = maps.shape
    batch = 2 if count % 2 == 0 else 1
    return pl.pallas_call(
        target_body,
        out_shape=[pltpu.HBM((count, rows, CW), jnp.float32), token_shape()],
        grid=(count // batch,),
        in_specs=[pl.BlockSpec((batch, 1, rows), lambda i: (i, 0, 0))] + untouched(1),
        out_specs=[pl.BlockSpec((batch, rows, CW), lambda i: (i, 0, 0)), token_spec()],
        compiler_params=params(16),
        cost_estimate=cost(count * rows * CW, 4 * count * rows * CW),
        name="sorted_targets",
    )(maps.reshape(count, 1, rows), earlier)


def coded_rows(value, out_ref):
    rows = value.shape[0]
    top = jnp.max(jnp.abs(value), axis=0, keepdims=True)
    exponent = jnp.floor(jnp.log2(jnp.maximum(top, 2.0**-108))) + 1.0
    code = jnp.floor(value * jnp.exp2(CODE_BITS - exponent) + 0.5).astype(jnp.int32)
    out_ref[:rows, :] = code.astype(jnp.int16)
    out_ref[rows:, :] = jnp.broadcast_to(exponent.astype(jnp.int32), (EXP_ROWS, CW)).astype(jnp.int16)


def update_body(count, odd_ref, pairs_ref, left_ref, projected_ref, contrib_ref, *refs):
    out_refs = refs[-2 * count :]
    joint, width = left_ref.shape
    rows = joint // 2
    odd = odd_ref[0] > 0
    for start in range(0, count, 2):
        span = min(2, count - start)
        part = projected_ref[:, :, start * CW : (start + span) * CW].reshape(width, span * CW)
        product = jnp.dot(left_ref[...], part, preferred_element_type=jnp.float32)
        for step in range(start, start + span):
            reduced = contrib_ref[pairs_ref[step]].astype(jnp.float32)
            reduced = reduced - product[:, (step - start) * CW : (step - start + 1) * CW]
            first, second = swapped(odd, *halves(reduced[:rows], reduced[rows:]))
            coded_rows(first, out_refs[2 * step])
            coded_rows(second, out_refs[2 * step + 1])


def update_group(odd, pairs, left, projected, contrib, earlier):
    joint, width = left.shape
    count = projected.shape[2] // CW
    return pl.pallas_call(
        functools.partial(update_body, count),
        out_shape=[pltpu.HBM((joint // 2 + EXP_ROWS, CW), jnp.int16)] * (2 * count),
        in_specs=[smem()] * 2 + [vmem()] * 3 + untouched(len(earlier)),
        out_specs=[vmem()] * (2 * count),
        compiler_params=params(28),
        cost_estimate=cost(2 * joint * width * count * CW, 2 * count * CW * (width + 2 * joint)),
        name="update_group",
    )(odd, pairs, left, projected, contrib, *earlier)


def scatter_body(count, has_partial, starts_ref, targets_ref, *refs):
    sources = refs[:count]
    partial_ref = refs[count] if has_partial else None
    out_ref, token_ref, values, one_hot = refs[-4:]
    joint = targets_ref.shape[1]
    rows = joint // 2

    @pl.when(pl.program_id(0) == 0)
    def _():
        for step in range(count):
            code = sources[step][:rows, :].astype(jnp.int32).astype(jnp.float32)
            exponent = sources[step][rows:, :].astype(jnp.int32).astype(jnp.float32)[:1]
            value = code * jnp.exp2(exponent - CODE_BITS)
            high = value.astype(jnp.bfloat16).astype(jnp.float32)
            low = value - high
            top, bottom = halves(high, low)
            values[step * joint : step * joint + rows, :] = top.astype(jnp.bfloat16)
            values[step * joint + rows : (step + 1) * joint, :] = bottom.astype(jnp.bfloat16)

    set_token(token_ref)
    lanes = lax.broadcasted_iota(jnp.int32, (WIN, rows), 1)
    batch = out_ref.shape[0]
    for place in range(batch):
        tile = pl.program_id(0) * batch + place
        lane = (lanes + tile * rows).astype(jnp.float32)
        parts = []
        for step in range(count):
            begin = jnp.minimum((starts_ref[step, tile] // 16) * 16, joint - WIN)
            begin = pl.multiple_of(begin, 16)
            target = targets_ref[step, pl.ds(begin, WIN), :]
            target = jnp.concatenate([target] * (rows // CW), axis=1)
            match = jnp.where(target == lane, 1.0, 0.0)
            one_hot[place, step * WIN : (step + 1) * WIN, :] = match.astype(jnp.bfloat16)
            parts.append(values[pl.ds(pl.multiple_of(step * joint + begin, 16), WIN), :])
        window = jnp.concatenate(parts, axis=0)
        total = lax.dot_general(
            window, one_hot[place], (((0,), (0,)), ((), ())), preferred_element_type=jnp.float32
        )
        total = total[:HALF] + total[HALF:]
        if has_partial:
            total = total + partial_ref[place]
        out_ref[place] = total.astype(out_ref.dtype)


def scatter_rows(starts, targets, coded, partial, out_dtype):
    count = len(coded)
    joint = targets.shape[1]
    rows = joint // 2
    tiles = starts.shape[1]
    batch = min(TILE_BATCH, tiles)
    has_partial = partial is not None
    tile_spec = pl.BlockSpec((batch, HALF, rows), lambda t: (t, 0, 0))
    whole = pl.BlockSpec((rows + EXP_ROWS, CW), lambda t: (0, 0))
    extra = [tile_spec] if has_partial else []
    operands = [partial] if has_partial else []
    return pl.pallas_call(
        functools.partial(scatter_body, count, has_partial),
        out_shape=[pltpu.HBM((tiles, HALF, rows), out_dtype), token_shape()],
        grid=(tiles // batch,),
        in_specs=[smem(), pl.BlockSpec(targets.shape, lambda t: (0, 0, 0))] + [whole] * count + extra,
        out_specs=[tile_spec, token_spec()],
        scratch_shapes=[
            pltpu.VMEM((count * joint, CW), jnp.bfloat16),
            pltpu.VMEM((batch, count * WIN, rows), jnp.bfloat16),
        ],
        compiler_params=params(36),
        cost_estimate=cost(2 * CW * count * WIN * rows * tiles, 8 * tiles * HALF * rows),
        name="scatter_rows",
    )(starts, targets, *coded, *operands)


def total_body(parts_ref, out_ref):
    sources, cols, rows = parts_ref.shape
    parts = parts_ref[...].astype(jnp.float32).reshape(sources // 2, 2, cols, rows)
    out_ref[...] = jnp.sum(parts, axis=0).reshape(2 * cols, rows).T


def total_rows(parts):
    sources, cols, rows = parts.shape
    return pl.pallas_call(
        total_body,
        out_shape=jax.ShapeDtypeStruct((rows, 2 * cols), jnp.float32),
        grid=(rows // CW,),
        in_specs=[pl.BlockSpec((sources, cols, CW), lambda i: (0, 0, i))],
        out_specs=pl.BlockSpec((CW, 2 * cols), lambda i: (i, 0)),
        compiler_params=params(6),
        cost_estimate=cost(sources * cols * rows, 2 * sources * cols * rows),
        name="total_rows",
    )(parts)


def per_device(
    rhs_pivot,
    block_pattern,
    diag_inverse,
    right_factor,
    left_factor,
    tile_ranks,
    contrib_rhs,
    parent_map,
):
    owner = lax.axis_index("owner")
    blk = lax.axis_index("blk")
    partners = lax.axis_size("blk")
    tiles = lax.axis_size("owner")
    ring = RING if tiles % RING == 0 else tiles
    inverse, right = diag_inverse[0], right_factor[0]
    rows = inverse.shape[0]
    groups = groups_of(partners // 2)
    all_pairs = jnp.bitwise_xor(blk // 2, jnp.array(sum(groups, []), jnp.int32))
    pairs = [jnp.bitwise_xor(blk // 2, jnp.array(group, jnp.int32)) for group in groups]
    offsets = [[2 * q + side for q in group for side in range(2)] for group in groups]
    fronts = [jnp.bitwise_xor(blk, jnp.array(ks, jnp.int32)) for ks in offsets]
    odd = (blk % 2).reshape(1)
    half = (owner % 2).reshape(1)
    second = ((owner + blk) % 2).reshape(1)

    def mate(tile, front):
        shift = front % 2
        place = (tile % ring + shift) ^ 1
        return tile // ring * ring + (place - shift) % ring

    across = [
        (tile * partners + front, mate(tile, front) * partners + front)
        for tile in range(tiles)
        for front in range(partners)
    ]

    def exchange(values, ks):
        steps = [[(i, i ^ k) for i in range(partners)] for k in ks]
        return [v if k == 0 else lax.ppermute(v, "blk", p) for v, k, p in zip(values, ks, steps)]

    def over_owner(value):
        return lax.all_to_all(value, "owner", split_axis=0, concat_axis=0, tiled=True)

    pattern = block_pattern.reshape(-1)
    masked, token = mask_all(rhs_pivot, pattern)
    front_rhs = lax.all_to_all(masked, "blk", split_axis=0, concat_axis=0, tiled=True)
    other_left = lax.ppermute(left_factor[0], ("owner", "blk"), across)
    kept, away = pack_contrib(half, contrib_rhs[0], token)
    got = lax.ppermute(away, ("owner", "blk"), across)

    ranks_here = lax.dynamic_index_in_dim(tile_ranks[0], owner, 1, keepdims=False)
    keep = jnp.arange(RK, dtype=jnp.int32)[None, :] < ranks_here[:, None]
    right_t = right_transposed(odd, right, keep.astype(jnp.float32).reshape(1, -1), ring)

    def tile_maps(tile):
        return lax.dynamic_slice_in_dim(parent_map, tile * rows, rows, 1)

    is_odd = (jnp.arange(partners) % 2 == 1)[:, None]
    other_maps = jnp.where(is_odd, tile_maps(mate(owner, 1)), tile_maps(mate(owner, 0)))
    maps = jnp.concatenate([tile_maps(owner), other_maps], axis=1)
    own_keys = lax.dynamic_index_in_dim(maps, blk, 0, keepdims=False).astype(jnp.float32)
    edges = (jnp.arange(tiles) * rows).astype(jnp.float32)
    ordered = jnp.sort(maps.astype(jnp.float32), axis=1)
    group_maps, starts = [], []
    for chosen in fronts:
        group_maps.append(jnp.take(ordered, chosen, axis=0))
        below = group_maps[-1][:, :, None] < edges[None, None, :]
        starts.append(jnp.sum(below.astype(jnp.int32), axis=1))

    solved, projected = [], []
    spread = [sorted_targets(keys, token) for keys in group_maps]
    ready = [later for _, later in spread] + [other_left, got]
    part, sent, _ = solve_group(pairs[0], odd, inverse, right_t, front_rhs, ring, ready)
    solved.append(part)
    projected.append(over_owner(sent))
    left, contrib, ready = sort_rows(second, own_keys, left_factor[0], other_left, kept, got)

    partial, token = None, None
    count = len(groups)
    for index in range(count):
        if index + 1 < count:
            part, sent, _ = solve_group(
                pairs[index + 1], odd, inverse, right_t, front_rhs, ring, [ready]
            )
            solved.append(part)
            projected.append(over_owner(sent))
        earlier = [] if partial is None else [token]
        coded = update_group(odd, pairs[index], left, projected[index], contrib, earlier)
        arrived = exchange(coded, offsets[index])
        dtype = jnp.float32 if index + 1 < count else jnp.bfloat16
        partial, token = scatter_rows(starts[index], spread[index][0], arrived, partial, dtype)
    parent_update = total_rows(over_owner(partial))
    pivot_solution = place_blocks(all_pairs, solved)
    return (pivot_solution, parent_update)


def solution(mesh):
    return jax.shard_map(
        per_device,
        mesh=mesh,
        in_specs=(
            P(None, "owner", "blk"),
            P(None, "owner", "blk"),
            P("blk", "owner", None),
            P("blk", "owner", None),
            P("blk", "owner", None),
            P("blk", None, None),
            P("blk", "owner", None),
            P(),
        ),
        out_specs=(P("blk", "owner", None), P("owner", "blk")),
        check_vma=False,
    )
```

```python
import functools

import jax
import jax.numpy as jnp
from jax import lax
from jax.experimental import pallas as pl
from jax.experimental.pallas import tpu as pltpu
from jax.sharding import PartitionSpec as P

RK = 64
CW = 128
WIN = 144
HALF = CW // 2
EXP_ROWS = 16
RING = 8
BATCH = 4
TILE_BATCH = 4
CODE_BITS = 14
MIB = 1024 * 1024


def vmem():
    return pl.BlockSpec(memory_space=pltpu.VMEM)


def smem():
    return pl.BlockSpec(memory_space=pltpu.SMEM)


def token_shape():
    return jax.ShapeDtypeStruct((8, CW), jnp.float32)


def token_spec():
    return pl.BlockSpec((8, CW), lambda *grid: (0, 0))


def set_token(token_ref):
    token_ref[...] = jnp.zeros_like(token_ref)


def untouched(count):
    return [pl.BlockSpec(memory_space=pltpu.HBM)] * count


def params(mib):
    return pltpu.CompilerParams(vmem_limit_bytes=mib * MIB)


def cost(flops, bytes_accessed):
    return pl.CostEstimate(flops=int(flops), bytes_accessed=int(bytes_accessed), transcendentals=0)


def groups_of(count):
    if count == 8:
        return [[4, 5, 2, 3], [6, 7, 1, 0]]
    return [list(range(count // 2, count)), list(range(count // 2))]


def halves(first, second):
    left = jnp.concatenate([first[:, :HALF], second[:, :HALF]], axis=1)
    right = jnp.concatenate([first[:, HALF:], second[:, HALF:]], axis=1)
    return left, right


def swapped(flag, first, second):
    return jnp.where(flag, second, first), jnp.where(flag, first, second)


def mask_body(pattern_ref, rhs_ref, out_ref, token_ref):
    for step in range(rhs_ref.shape[0]):
        front = pl.program_id(0) * rhs_ref.shape[0] + step
        keep = pattern_ref[front].astype(jnp.float32)
        out_ref[step] = (rhs_ref[step].astype(jnp.float32) * keep).astype(jnp.bfloat16)
    set_token(token_ref)


def mask_all(rhs, pattern):
    count, rows, cols = rhs.shape
    spec = pl.BlockSpec((4, rows, cols), lambda i: (i, 0, 0))
    return pl.pallas_call(
        mask_body,
        out_shape=[pltpu.HBM(rhs.shape, jnp.bfloat16), token_shape()],
        grid=(count // 4,),
        in_specs=[smem(), spec],
        out_specs=[spec, token_spec()],
        compiler_params=params(60),
        cost_estimate=cost(count * rows * cols, 4 * count * rows * cols),
        name="mask_all",
    )(pattern, rhs)


def right_body(ring, odd_ref, right_ref, keep_ref, out_ref):
    kept = (right_ref[...].astype(jnp.float32) * keep_ref[...]).T
    span = ring * RK
    pieces = []
    for begin in range(0, kept.shape[0], span):
        pieces += [kept[begin + RK : begin + span], kept[begin : begin + RK]]
    turned = jnp.concatenate(pieces, axis=0)
    out_ref[...] = jnp.where(odd_ref[0] > 0, turned, kept).astype(jnp.bfloat16)


def right_transposed(odd, right, keep, ring):
    rows, width = right.shape
    return pl.pallas_call(
        functools.partial(right_body, ring),
        out_shape=pltpu.HBM((width, rows), jnp.bfloat16),
        in_specs=[smem()] + [vmem()] * 2,
        out_specs=vmem(),
        compiler_params=params(16),
        cost_estimate=cost(rows * width, 4 * rows * width),
        name="right_transposed",
    )(odd, right, keep)


def solve_body(count, ring, pairs_ref, odd_ref, inverse_ref, right_ref, *refs):
    sources = refs[:count]
    solved_ref, projected_ref, token_ref = refs[-3:]
    set_token(token_ref)
    depth = projected_ref.shape[0]
    odd = odd_ref[0]
    for step in range(count):
        block = jnp.concatenate(halves(sources[step][0], sources[step][1]), axis=1)
        solved = jnp.dot(inverse_ref[...], block, preferred_element_type=jnp.float32)
        solved = solved.astype(jnp.bfloat16)
        solved_ref[step, 0], solved_ref[step, 1] = halves(solved[:, :CW], solved[:, CW:])
        projected = jnp.dot(right_ref[...], solved, preferred_element_type=jnp.float32)
        projected = projected.astype(jnp.bfloat16)
        span = slice(step * CW, (step + 1) * CW)
        for begin in range(0, depth, ring):
            for tile in range(0, ring, 2):
                row = (begin + tile) * RK
                pair = projected[row : row + 2 * RK]
                projected_ref[begin + tile + 1, :, span] = pair[:, CW:]
                projected_ref[begin + lax.rem(tile + 2 * odd, ring), :, span] = pair[:, :CW]


def solve_group(pairs, odd, inverse, right, blocks, ring, earlier):
    count = pairs.shape[0]
    rows = inverse.shape[0]
    width = right.shape[0]
    depth = width // RK

    def whole(shape):
        return pl.BlockSpec(shape, lambda i, pairs_ref, odd_ref: (0,) * len(shape))

    def pick(step):
        return lambda i, pairs_ref, odd_ref: (pairs_ref[step], 0, 0)

    return pl.pallas_call(
        functools.partial(solve_body, count, ring),
        out_shape=[
            pltpu.HBM((count, 2, rows, CW), jnp.bfloat16),
            pltpu.HBM((depth, 2 * RK, count * CW), jnp.bfloat16),
            token_shape(),
        ],
        grid_spec=pltpu.PrefetchScalarGridSpec(
            num_scalar_prefetch=2,
            grid=(1,),
            in_specs=[whole((rows, rows)), whole((width, rows))]
            + [pl.BlockSpec((2, rows, CW), pick(step)) for step in range(count)]
            + untouched(len(earlier)),
            out_specs=[
                whole((count, 2, rows, CW)),
                whole((depth, 2 * RK, count * CW)),
                token_spec(),
            ],
        ),
        compiler_params=params(20),
        cost_estimate=cost(4 * rows * (rows + width) * count * CW, 4 * count * CW * (2 * rows + width)),
        name="solve_group",
    )(pairs, odd, inverse, right, *([blocks] * count), *earlier)


def place_body(starts, pairs_ref, *refs):
    out_ref = refs[-1]
    step = pl.program_id(0)
    for begin, end, ref in zip(starts[:-1], starts[1:], refs[:-1]):

        @pl.when((step >= begin) & (step < end))
        def _(ref=ref):
            out_ref[0, :, :CW] = ref[0, 0]
            out_ref[0, :, CW:] = ref[0, 1]


def place_blocks(pairs, parts):
    starts = [0]
    for part in parts:
        starts.append(starts[-1] + part.shape[0])
    rows = parts[0].shape[2]

    def pick(begin, end):
        return lambda i, pairs_ref: (jnp.clip(i - begin, 0, end - begin - 1), 0, 0, 0)

    return pl.pallas_call(
        functools.partial(place_body, starts),
        out_shape=jax.ShapeDtypeStruct((1, rows, starts[-1] * 2 * CW), jnp.bfloat16),
        grid_spec=pltpu.PrefetchScalarGridSpec(
            num_scalar_prefetch=1,
            grid=(starts[-1],),
            in_specs=[
                pl.BlockSpec((1, 2, rows, CW), pick(begin, end))
                for begin, end in zip(starts[:-1], starts[1:])
            ],
            out_specs=pl.BlockSpec((1, rows, 2 * CW), lambda i, pairs_ref: (0, 0, pairs_ref[i])),
        ),
        compiler_params=params(6),
        cost_estimate=cost(0, 8 * rows * starts[-1] * CW),
        name="place_blocks",
    )(pairs, *parts)


def pack_body(high_ref, contrib_ref, after_ref, keep_ref, send_ref):
    high = high_ref[0] > 0
    for step in range(keep_ref.shape[1] // CW):
        even = contrib_ref[:, 2 * step * CW : (2 * step + 1) * CW]
        other = contrib_ref[:, (2 * step + 1) * CW : (2 * step + 2) * CW]
        span = slice(step * CW, (step + 1) * CW)
        keep_ref[:, span], send_ref[:, span] = swapped(high, *halves(even, other))


def pack_contrib(high, contrib, earlier):
    rows, cols = contrib.shape
    spec = pl.BlockSpec((rows, cols // 4), lambda i: (0, i))
    return pl.pallas_call(
        pack_body,
        out_shape=[pltpu.HBM((rows, cols // 2), jnp.bfloat16)] * 2,
        grid=(2,),
        in_specs=[smem(), pl.BlockSpec((rows, cols // 2), lambda i: (0, i))] + untouched(1),
        out_specs=[spec] * 2,
        compiler_params=params(60),
        cost_estimate=cost(0, MIB),
        name="pack_contrib",
    )(high, contrib, earlier)


def ordering(keys):
    rows = keys.shape[1]
    column = jnp.broadcast_to(keys, (CW, rows)).T
    smaller = (jnp.concatenate([column] * (rows // CW), axis=1) < keys).astype(jnp.float32)
    rank = jnp.sum(smaller, axis=0, keepdims=True)
    place = lax.broadcasted_iota(jnp.int32, (rows, rows), 0).astype(jnp.float32)
    return jnp.where(place == rank, 1.0, 0.0).astype(jnp.bfloat16)


def sort_body(
    high_ref, keys_ref, own_ref, other_ref, kept_ref, got_ref, left_out, contrib_out, token_ref, one_hot
):
    rows = own_ref.shape[0]

    @pl.when(pl.program_id(0) == 0)
    def _():
        one_hot[...] = ordering(keys_ref[...])
        set_token(token_ref)

    def sort(value, begin):
        order = one_hot[:, begin : begin + rows]
        return jnp.dot(order, value, preferred_element_type=jnp.float32)

    own, other = sort(own_ref[...], 0), sort(other_ref[...], rows)
    low, top = swapped(high_ref[0] > 0, own, other)
    for step in range(low.shape[1] // CW):
        span = slice(step * CW, (step + 1) * CW)
        pair = halves(low[:, span], top[:, span])
        left_out[:, 2 * step * CW : (2 * step + 1) * CW] = pair[0].astype(jnp.bfloat16)
        left_out[:, (2 * step + 1) * CW : (2 * step + 2) * CW] = pair[1].astype(jnp.bfloat16)

    contrib = sort(kept_ref[...], 0) + sort(got_ref[...], rows)
    for step in range(contrib_out.shape[0]):
        contrib_out[step] = contrib[:, step * CW : (step + 1) * CW].astype(jnp.bfloat16)


def sort_rows(high, keys, own, other, kept, got):
    rows, width = own.shape
    cols = kept.shape[1]
    joint = 2 * rows
    steps = min(4, cols // CW)
    spread = min(steps, width // CW)
    return pl.pallas_call(
        sort_body,
        out_shape=[
            pltpu.HBM((joint, 2 * width), jnp.bfloat16),
            pltpu.HBM((cols // CW, joint, CW), jnp.bfloat16),
            token_shape(),
        ],
        grid=(steps,),
        in_specs=[
            smem(),
            pl.BlockSpec((1, joint), lambda i: (0, 0)),
            pl.BlockSpec((rows, width // spread), lambda i: (0, i % spread)),
            pl.BlockSpec((rows, width // spread), lambda i: (0, i % spread)),
            pl.BlockSpec((rows, cols // steps), lambda i: (0, i)),
            pl.BlockSpec((rows, cols // steps), lambda i: (0, i)),
        ],
        out_specs=[
            pl.BlockSpec((joint, 2 * width // spread), lambda i: (0, i % spread)),
            pl.BlockSpec((cols // CW // steps, joint, CW), lambda i: (i, 0, 0)),
            token_spec(),
        ],
        scratch_shapes=[pltpu.VMEM((joint, joint), jnp.bfloat16)],
        compiler_params=params(28),
        cost_estimate=cost(2 * joint * rows * (2 * width + 2 * cols), 8 * rows * (width + cols)),
        name="sort_rows",
    )(high, keys.reshape(1, joint), own, other, kept, got)


def target_body(keys_ref, after_ref, out_ref, token_ref):
    for step in range(keys_ref.shape[0]):
        keys = keys_ref[step]
        out_ref[step] = jnp.broadcast_to(keys, (CW, keys.shape[1])).T
    set_token(token_ref)


def sorted_targets(maps, earlier):
    count, rows = maps.shape
    batch = 2 if count % 2 == 0 else 1
    return pl.pallas_call(
        target_body,
        out_shape=[pltpu.HBM((count, rows, CW), jnp.float32), token_shape()],
        grid=(count // batch,),
        in_specs=[pl.BlockSpec((batch, 1, rows), lambda i: (i, 0, 0))] + untouched(1),
        out_specs=[pl.BlockSpec((batch, rows, CW), lambda i: (i, 0, 0)), token_spec()],
        compiler_params=params(16),
        cost_estimate=cost(0, MIB),
        name="sorted_targets",
    )(maps.reshape(count, 1, rows), earlier)


def coded_rows(value, out_ref):
    rows = value.shape[0]
    top = jnp.max(jnp.abs(value), axis=0, keepdims=True)
    exponent = jnp.floor(jnp.log2(jnp.maximum(top, 2.0**-108))) + 1.0
    code = jnp.floor(value * jnp.exp2(CODE_BITS - exponent) + 0.5).astype(jnp.int32)
    out_ref[:rows, :] = code.astype(jnp.int16)
    out_ref[rows:, :] = jnp.broadcast_to(exponent.astype(jnp.int32), (EXP_ROWS, CW)).astype(jnp.int16)


def update_body(count, pairs_ref, odd_ref, left_ref, projected_ref, *refs):
    contribs = refs[:count]
    out_refs = refs[-2 * count :]
    joint, width = left_ref.shape
    rows = joint // 2
    part = projected_ref[...].reshape(width, count * CW)
    product = jnp.dot(left_ref[...], part, preferred_element_type=jnp.float32)
    for step in range(count):
        reduced = contribs[step][0].astype(jnp.float32) - product[:, step * CW : (step + 1) * CW]
        sides = swapped(odd_ref[0] > 0, *halves(reduced[:rows], reduced[rows:]))
        coded_rows(sides[0], out_refs[2 * step])
        coded_rows(sides[1], out_refs[2 * step + 1])


def update_group(odd, pairs, left, projected, place, contrib, earlier):
    joint, width = left.shape
    depth = projected.shape[0]
    count = pairs.shape[0]
    coded = (joint // 2 + EXP_ROWS, CW)

    def pick(step):
        return lambda i, pairs_ref, odd_ref: (pairs_ref[step], 0, 0)

    return pl.pallas_call(
        functools.partial(update_body, count),
        out_shape=[pltpu.HBM(coded, jnp.int16)] * (2 * count),
        grid_spec=pltpu.PrefetchScalarGridSpec(
            num_scalar_prefetch=2,
            grid=(1,),
            in_specs=[
                pl.BlockSpec((joint, width), lambda i, a, b: (0, 0)),
                pl.BlockSpec((depth, 2 * RK, count * CW), lambda i, a, b: (0, 0, place)),
            ]
            + [pl.BlockSpec((1, joint, CW), pick(step)) for step in range(count)]
            + untouched(len(earlier)),
            out_specs=[pl.BlockSpec(coded, lambda i, a, b: (0, 0))] * (2 * count),
        ),
        compiler_params=params(28),
        cost_estimate=cost(2 * joint * width * count * CW, 2 * count * CW * (width + 2 * joint)),
        name="update_group",
    )(pairs, odd, left, projected, *([contrib] * count), *earlier)


def scatter_body(count, has_partial, starts_ref, targets_ref, *refs):
    sources = refs[:count]
    partial_ref = refs[count] if has_partial else None
    out_ref, token_ref, values, one_hot = refs[-4:]
    joint = targets_ref.shape[1]
    rows = joint // 2

    @pl.when(pl.program_id(0) == 0)
    def _():
        for step in range(count):
            code = sources[step][:rows, :].astype(jnp.int32).astype(jnp.float32)
            exponent = sources[step][rows:, :].astype(jnp.int32).astype(jnp.float32)[:1]
            value = code * jnp.exp2(exponent - CODE_BITS)
            high = value.astype(jnp.bfloat16).astype(jnp.float32)
            low = value - high
            top, bottom = halves(high, low)
            values[step * joint : step * joint + rows, :] = top.astype(jnp.bfloat16)
            values[step * joint + rows : (step + 1) * joint, :] = bottom.astype(jnp.bfloat16)

    set_token(token_ref)
    lanes = lax.broadcasted_iota(jnp.int32, (WIN, rows), 1)
    batch = out_ref.shape[0]
    for place in range(batch):
        tile = pl.program_id(0) * batch + place
        lane = (lanes + tile * rows).astype(jnp.float32)
        parts = []
        for step in range(count):
            begin = jnp.minimum((starts_ref[step, tile] // 16) * 16, joint - WIN)
            begin = pl.multiple_of(begin, 16)
            target = targets_ref[step, pl.ds(begin, WIN), :]
            target = jnp.concatenate([target] * (rows // CW), axis=1)
            match = jnp.where(target == lane, 1.0, 0.0)
            one_hot[place, step * WIN : (step + 1) * WIN, :] = match.astype(jnp.bfloat16)
            parts.append(values[pl.ds(pl.multiple_of(step * joint + begin, 16), WIN), :])
        window = jnp.concatenate(parts, axis=0)
        total = lax.dot_general(
            window, one_hot[place], (((0,), (0,)), ((), ())), preferred_element_type=jnp.float32
        )
        total = total[:HALF] + total[HALF:]
        if has_partial:
            total = total + partial_ref[place]
        out_ref[place] = total.astype(out_ref.dtype)


def scatter_rows(starts, targets, coded, partial, out_dtype):
    count = len(coded)
    joint = targets.shape[1]
    rows = joint // 2
    tiles = starts.shape[1]
    batch = min(TILE_BATCH, tiles)
    has_partial = partial is not None
    tile_spec = pl.BlockSpec((batch, HALF, rows), lambda t: (t, 0, 0))
    whole = pl.BlockSpec((rows + EXP_ROWS, CW), lambda t: (0, 0))
    extra = [tile_spec] if has_partial else []
    operands = [partial] if has_partial else []
    return pl.pallas_call(
        functools.partial(scatter_body, count, has_partial),
        out_shape=[pltpu.HBM((tiles, HALF, rows), out_dtype), token_shape()],
        grid=(tiles // batch,),
        in_specs=[smem(), pl.BlockSpec(targets.shape, lambda t: (0, 0, 0))] + [whole] * count + extra,
        out_specs=[tile_spec, token_spec()],
        scratch_shapes=[
            pltpu.VMEM((count * joint, CW), jnp.bfloat16),
            pltpu.VMEM((batch, count * WIN, rows), jnp.bfloat16),
        ],
        compiler_params=params(36),
        cost_estimate=cost(2 * CW * count * WIN * rows * tiles, 8 * tiles * HALF * rows),
        name="scatter_rows",
    )(starts, targets, *coded, *operands)


def total_body(parts_ref, out_ref):
    sources, cols, rows = parts_ref.shape
    parts = parts_ref[...].astype(jnp.float32).reshape(sources // 2, 2, cols, rows)
    out_ref[...] = jnp.sum(parts, axis=0).reshape(2 * cols, rows).T


def total_rows(parts):
    sources, cols, rows = parts.shape
    return pl.pallas_call(
        total_body,
        out_shape=jax.ShapeDtypeStruct((rows, 2 * cols), jnp.float32),
        grid=(rows // CW,),
        in_specs=[pl.BlockSpec((sources, cols, CW), lambda i: (0, 0, i))],
        out_specs=pl.BlockSpec((CW, 2 * cols), lambda i: (i, 0)),
        compiler_params=params(6),
        cost_estimate=cost(sources * cols * rows, 2 * sources * cols * rows),
        name="total_rows",
    )(parts)


def per_device(
    rhs_pivot,
    block_pattern,
    diag_inverse,
    right_factor,
    left_factor,
    tile_ranks,
    contrib_rhs,
    parent_map,
):
    owner = lax.axis_index("owner")
    blk = lax.axis_index("blk")
    partners = lax.axis_size("blk")
    tiles = lax.axis_size("owner")
    ring = RING if tiles % RING == 0 else tiles
    inverse, right = diag_inverse[0], right_factor[0]
    rows = inverse.shape[0]
    groups = groups_of(partners // 2)
    all_pairs = jnp.bitwise_xor(blk // 2, jnp.array(sum(groups, []), jnp.int32))
    pairs = [jnp.bitwise_xor(blk // 2, jnp.array(group, jnp.int32)) for group in groups]
    batches = [
        [group[begin : begin + BATCH] for begin in range(0, len(group), BATCH)] for group in groups
    ]
    offsets = {
        tuple(batch): [2 * q + side for q in batch for side in range(2)]
        for group in batches
        for batch in group
    }
    fronts = [
        jnp.bitwise_xor(blk, jnp.array(sum((offsets[tuple(b)] for b in group), []), jnp.int32))
        for group in batches
    ]
    odd = (blk % 2).reshape(1)
    half = (owner % 2).reshape(1)
    second = ((owner + blk) % 2).reshape(1)

    def mate(tile, front):
        shift = front % 2
        place = (tile % ring + shift) ^ 1
        return tile // ring * ring + (place - shift) % ring

    across = [
        (tile * partners + front, mate(tile, front) * partners + front)
        for tile in range(tiles)
        for front in range(partners)
    ]

    def exchange(values, ks):
        steps = [[(i, i ^ k) for i in range(partners)] for k in ks]
        return [v if k == 0 else lax.ppermute(v, "blk", p) for v, k, p in zip(values, ks, steps)]

    def over_owner(value):
        return lax.all_to_all(value, "owner", split_axis=0, concat_axis=0, tiled=True)

    pattern = block_pattern.reshape(-1)
    masked, token = mask_all(rhs_pivot, pattern)
    front_rhs = lax.all_to_all(masked, "blk", split_axis=0, concat_axis=0, tiled=True)
    other_left = lax.ppermute(left_factor[0], ("owner", "blk"), across)
    kept, away = pack_contrib(half, contrib_rhs[0], token)
    got = lax.ppermute(away, ("owner", "blk"), across)

    ranks_here = lax.dynamic_index_in_dim(tile_ranks[0], owner, 1, keepdims=False)
    keep = jnp.arange(RK, dtype=jnp.int32)[None, :] < ranks_here[:, None]
    right_t = right_transposed(odd, right, keep.astype(jnp.float32).reshape(1, -1), ring)

    def tile_maps(tile):
        return lax.dynamic_slice_in_dim(parent_map, tile * rows, rows, 1)

    is_odd = (jnp.arange(partners) % 2 == 1)[:, None]
    other_maps = jnp.where(is_odd, tile_maps(mate(owner, 1)), tile_maps(mate(owner, 0)))
    maps = jnp.concatenate([tile_maps(owner), other_maps], axis=1)
    own_keys = lax.dynamic_index_in_dim(maps, blk, 0, keepdims=False).astype(jnp.float32)
    edges = (jnp.arange(tiles) * rows).astype(jnp.float32)
    ordered = jnp.sort(maps.astype(jnp.float32), axis=1)
    group_maps, starts = [], []
    for chosen in fronts:
        group_maps.append(jnp.take(ordered, chosen, axis=0))
        below = group_maps[-1][:, :, None] < edges[None, None, :]
        starts.append(jnp.sum(below.astype(jnp.int32), axis=1))

    solved, projected = [], []
    spread = [sorted_targets(keys, token) for keys in group_maps]
    ready = [later for _, later in spread] + [other_left, got]
    part, sent, _ = solve_group(pairs[0], odd, inverse, right_t, front_rhs, ring, ready)
    solved.append(part)
    projected.append(over_owner(sent))
    left, contrib, ready = sort_rows(second, own_keys, left_factor[0], other_left, kept, got)

    partial, token = None, None
    count = len(groups)
    for index in range(count):
        if index + 1 < count:
            part, sent, _ = solve_group(
                pairs[index + 1], odd, inverse, right_t, front_rhs, ring, [ready]
            )
            solved.append(part)
            projected.append(over_owner(sent))
        earlier = [] if partial is None else [token]
        arrived = []
        for place, batch in enumerate(batches[index]):
            chosen = jnp.bitwise_xor(blk // 2, jnp.array(batch, jnp.int32))
            coded = update_group(odd, chosen, left, projected[index], place, contrib, earlier)
            arrived += exchange(coded, offsets[tuple(batch)])
        dtype = jnp.float32 if index + 1 < count else jnp.bfloat16
        partial, token = scatter_rows(starts[index], spread[index][0], arrived, partial, dtype)
    parent_update = total_rows(over_owner(partial))
    pivot_solution = place_blocks(all_pairs, solved)
    return (pivot_solution, parent_update)


def solution(mesh):
    return jax.shard_map(
        per_device,
        mesh=mesh,
        in_specs=(
            P(None, "owner", "blk"),
            P(None, "owner", "blk"),
            P("blk", "owner", None),
            P("blk", "owner", None),
            P("blk", "owner", None),
            P("blk", None, None),
            P("blk", "owner", None),
            P(),
        ),
        out_specs=(P("blk", "owner", None), P("owner", "blk")),
        check_vma=False,
    )
```

```python
import functools

import jax
import jax.numpy as jnp
from jax import lax
from jax.experimental import pallas as pl
from jax.experimental.pallas import tpu as pltpu
from jax.sharding import PartitionSpec as P

RK = 64
CW = 128
WIN = 144
HALF = CW // 2
EXP_ROWS = 16
RING = 8
BATCH = 4
TILE_BATCH = 8
CODE_BITS = 14
MIB = 1024 * 1024


def vmem():
    return pl.BlockSpec(memory_space=pltpu.VMEM)


def smem():
    return pl.BlockSpec(memory_space=pltpu.SMEM)


def token_shape():
    return jax.ShapeDtypeStruct((8, CW), jnp.float32)


def token_spec():
    return pl.BlockSpec((8, CW), lambda *grid: (0, 0))


def set_token(token_ref):
    token_ref[...] = jnp.zeros_like(token_ref)


def untouched(count):
    return [pl.BlockSpec(memory_space=pltpu.HBM)] * count


def params(mib):
    return pltpu.CompilerParams(vmem_limit_bytes=mib * MIB)


def cost(flops, bytes_accessed):
    return pl.CostEstimate(flops=int(flops), bytes_accessed=int(bytes_accessed), transcendentals=0)


def groups_of(count):
    if count == 8:
        return [[4, 6, 2, 3], [5, 7, 1, 0]]
    return [list(range(count // 2, count)), list(range(count // 2))]


def halves(first, second):
    left = jnp.concatenate([first[:, :HALF], second[:, :HALF]], axis=1)
    right = jnp.concatenate([first[:, HALF:], second[:, HALF:]], axis=1)
    return left, right


def swapped(flag, first, second):
    return jnp.where(flag, second, first), jnp.where(flag, first, second)


def mask_body(pattern_ref, rhs_ref, out_ref, token_ref):
    for step in range(rhs_ref.shape[0]):
        front = pl.program_id(0) * rhs_ref.shape[0] + step
        keep = pattern_ref[front].astype(jnp.float32)
        out_ref[step] = (rhs_ref[step].astype(jnp.float32) * keep).astype(jnp.bfloat16)
    set_token(token_ref)


def mask_all(rhs, pattern):
    count, rows, cols = rhs.shape
    spec = pl.BlockSpec((4, rows, cols), lambda i: (i, 0, 0))
    return pl.pallas_call(
        mask_body,
        out_shape=[pltpu.HBM(rhs.shape, jnp.bfloat16), token_shape()],
        grid=(count // 4,),
        in_specs=[smem(), spec],
        out_specs=[spec, token_spec()],
        compiler_params=params(60),
        cost_estimate=cost(count * rows * cols, 4 * count * rows * cols),
        name="mask_all",
    )(pattern, rhs)


def right_body(ring, odd_ref, right_ref, keep_ref, out_ref):
    kept = (right_ref[...].astype(jnp.float32) * keep_ref[...]).T
    span = ring * RK
    pieces = []
    for begin in range(0, kept.shape[0], span):
        pieces += [kept[begin + RK : begin + span], kept[begin : begin + RK]]
    turned = jnp.concatenate(pieces, axis=0)
    out_ref[...] = jnp.where(odd_ref[0] > 0, turned, kept).astype(jnp.bfloat16)


def right_transposed(odd, right, keep, ring):
    rows, width = right.shape
    return pl.pallas_call(
        functools.partial(right_body, ring),
        out_shape=pltpu.HBM((width, rows), jnp.bfloat16),
        in_specs=[smem()] + [vmem()] * 2,
        out_specs=vmem(),
        compiler_params=params(16),
        cost_estimate=cost(rows * width, 4 * rows * width),
        name="right_transposed",
    )(odd, right, keep)


def solve_body(count, ring, pairs_ref, odd_ref, inverse_ref, right_ref, *refs):
    sources = refs[:count]
    solved_ref, projected_ref, token_ref = refs[-3:]
    set_token(token_ref)
    depth = projected_ref.shape[0]
    odd = odd_ref[0]
    for step in range(count):
        block = jnp.concatenate(halves(sources[step][0], sources[step][1]), axis=1)
        solved = jnp.dot(inverse_ref[...], block, preferred_element_type=jnp.float32)
        solved = solved.astype(jnp.bfloat16)
        solved_ref[step, 0], solved_ref[step, 1] = halves(solved[:, :CW], solved[:, CW:])
        projected = jnp.dot(right_ref[...], solved, preferred_element_type=jnp.float32)
        projected = projected.astype(jnp.bfloat16)
        span = slice(step * CW, (step + 1) * CW)
        for begin in range(0, depth, ring):
            for tile in range(0, ring, 2):
                row = (begin + tile) * RK
                pair = projected[row : row + 2 * RK]
                projected_ref[begin + tile + 1, :, span] = pair[:, CW:]
                projected_ref[begin + lax.rem(tile + 2 * odd, ring), :, span] = pair[:, :CW]


def solve_group(pairs, odd, inverse, right, blocks, ring, earlier):
    count = pairs.shape[0]
    rows = inverse.shape[0]
    width = right.shape[0]
    depth = width // RK

    def whole(shape):
        return pl.BlockSpec(shape, lambda i, pairs_ref, odd_ref: (0,) * len(shape))

    def pick(step):
        return lambda i, pairs_ref, odd_ref: (pairs_ref[step], 0, 0)

    return pl.pallas_call(
        functools.partial(solve_body, count, ring),
        out_shape=[
            pltpu.HBM((count, 2, rows, CW), jnp.bfloat16),
            pltpu.HBM((depth, 2 * RK, count * CW), jnp.bfloat16),
            token_shape(),
        ],
        grid_spec=pltpu.PrefetchScalarGridSpec(
            num_scalar_prefetch=2,
            grid=(1,),
            in_specs=[whole((rows, rows)), whole((width, rows))]
            + [pl.BlockSpec((2, rows, CW), pick(step)) for step in range(count)]
            + untouched(len(earlier)),
            out_specs=[
                whole((count, 2, rows, CW)),
                whole((depth, 2 * RK, count * CW)),
                token_spec(),
            ],
        ),
        compiler_params=params(20),
        cost_estimate=cost(4 * rows * (rows + width) * count * CW, 4 * count * CW * (2 * rows + width)),
        name="solve_group",
    )(pairs, odd, inverse, right, *([blocks] * count), *earlier)


def place_body(starts, pairs_ref, *refs):
    out_ref = refs[-1]
    step = pl.program_id(0)
    for begin, end, ref in zip(starts[:-1], starts[1:], refs[:-1]):

        @pl.when((step >= begin) & (step < end))
        def _(ref=ref):
            out_ref[0, :, :CW] = ref[0, 0]
            out_ref[0, :, CW:] = ref[0, 1]


def place_blocks(pairs, parts):
    starts = [0]
    for part in parts:
        starts.append(starts[-1] + part.shape[0])
    rows = parts[0].shape[2]

    def pick(begin, end):
        return lambda i, pairs_ref: (jnp.clip(i - begin, 0, end - begin - 1), 0, 0, 0)

    return pl.pallas_call(
        functools.partial(place_body, starts),
        out_shape=jax.ShapeDtypeStruct((1, rows, starts[-1] * 2 * CW), jnp.bfloat16),
        grid_spec=pltpu.PrefetchScalarGridSpec(
            num_scalar_prefetch=1,
            grid=(starts[-1],),
            in_specs=[
                pl.BlockSpec((1, 2, rows, CW), pick(begin, end))
                for begin, end in zip(starts[:-1], starts[1:])
            ],
            out_specs=pl.BlockSpec((1, rows, 2 * CW), lambda i, pairs_ref: (0, 0, pairs_ref[i])),
        ),
        compiler_params=params(6),
        cost_estimate=cost(0, 8 * rows * starts[-1] * CW),
        name="place_blocks",
    )(pairs, *parts)


def pack_body(high_ref, contrib_ref, after_ref, keep_ref, send_ref):
    high = high_ref[0] > 0
    for step in range(keep_ref.shape[1] // CW):
        even = contrib_ref[:, 2 * step * CW : (2 * step + 1) * CW]
        other = contrib_ref[:, (2 * step + 1) * CW : (2 * step + 2) * CW]
        span = slice(step * CW, (step + 1) * CW)
        keep_ref[:, span], send_ref[:, span] = swapped(high, *halves(even, other))


def pack_contrib(high, contrib, earlier):
    rows, cols = contrib.shape
    spec = pl.BlockSpec((rows, cols // 4), lambda i: (0, i))
    return pl.pallas_call(
        pack_body,
        out_shape=[pltpu.HBM((rows, cols // 2), jnp.bfloat16)] * 2,
        grid=(2,),
        in_specs=[smem(), pl.BlockSpec((rows, cols // 2), lambda i: (0, i))] + untouched(1),
        out_specs=[spec] * 2,
        compiler_params=params(60),
        cost_estimate=cost(0, MIB),
        name="pack_contrib",
    )(high, contrib, earlier)


def ordering(keys):
    rows = keys.shape[1]
    column = jnp.broadcast_to(keys, (CW, rows)).T
    smaller = (jnp.concatenate([column] * (rows // CW), axis=1) < keys).astype(jnp.float32)
    rank = jnp.sum(smaller, axis=0, keepdims=True)
    place = lax.broadcasted_iota(jnp.int32, (rows, rows), 0).astype(jnp.float32)
    return jnp.where(place == rank, 1.0, 0.0).astype(jnp.bfloat16)


def sort_body(
    high_ref, keys_ref, own_ref, other_ref, kept_ref, got_ref, left_out, contrib_out, token_ref, one_hot
):
    rows = own_ref.shape[0]

    @pl.when(pl.program_id(0) == 0)
    def _():
        one_hot[...] = ordering(keys_ref[...])
        set_token(token_ref)

    def sort(value, begin):
        order = one_hot[:, begin : begin + rows]
        return jnp.dot(order, value, preferred_element_type=jnp.float32)

    own, other = sort(own_ref[...], 0), sort(other_ref[...], rows)
    low, top = swapped(high_ref[0] > 0, own, other)
    for step in range(low.shape[1] // CW):
        span = slice(step * CW, (step + 1) * CW)
        pair = halves(low[:, span], top[:, span])
        left_out[:, 2 * step * CW : (2 * step + 1) * CW] = pair[0].astype(jnp.bfloat16)
        left_out[:, (2 * step + 1) * CW : (2 * step + 2) * CW] = pair[1].astype(jnp.bfloat16)

    contrib = sort(kept_ref[...], 0) + sort(got_ref[...], rows)
    for step in range(contrib_out.shape[0]):
        contrib_out[step] = contrib[:, step * CW : (step + 1) * CW].astype(jnp.bfloat16)


def sort_rows(high, keys, own, other, kept, got):
    rows, width = own.shape
    cols = kept.shape[1]
    joint = 2 * rows
    steps = min(4, cols // CW)
    spread = min(steps, width // CW)
    return pl.pallas_call(
        sort_body,
        out_shape=[
            pltpu.HBM((joint, 2 * width), jnp.bfloat16),
            pltpu.HBM((cols // CW, joint, CW), jnp.bfloat16),
            token_shape(),
        ],
        grid=(steps,),
        in_specs=[
            smem(),
            pl.BlockSpec((1, joint), lambda i: (0, 0)),
            pl.BlockSpec((rows, width // spread), lambda i: (0, i % spread)),
            pl.BlockSpec((rows, width // spread), lambda i: (0, i % spread)),
            pl.BlockSpec((rows, cols // steps), lambda i: (0, i)),
            pl.BlockSpec((rows, cols // steps), lambda i: (0, i)),
        ],
        out_specs=[
            pl.BlockSpec((joint, 2 * width // spread), lambda i: (0, i % spread)),
            pl.BlockSpec((cols // CW // steps, joint, CW), lambda i: (i, 0, 0)),
            token_spec(),
        ],
        scratch_shapes=[pltpu.VMEM((joint, joint), jnp.bfloat16)],
        compiler_params=params(28),
        cost_estimate=cost(2 * joint * rows * (2 * width + 2 * cols), 8 * rows * (width + cols)),
        name="sort_rows",
    )(high, keys.reshape(1, joint), own, other, kept, got)


def target_body(keys_ref, after_ref, out_ref, token_ref):
    for step in range(keys_ref.shape[0]):
        keys = keys_ref[step]
        out_ref[step] = jnp.broadcast_to(keys, (CW, keys.shape[1])).T
    set_token(token_ref)


def sorted_targets(maps, earlier):
    count, rows = maps.shape
    batch = 2 if count % 2 == 0 else 1
    return pl.pallas_call(
        target_body,
        out_shape=[pltpu.HBM((count, rows, CW), jnp.float32), token_shape()],
        grid=(count // batch,),
        in_specs=[pl.BlockSpec((batch, 1, rows), lambda i: (i, 0, 0))] + untouched(1),
        out_specs=[pl.BlockSpec((batch, rows, CW), lambda i: (i, 0, 0)), token_spec()],
        compiler_params=params(16),
        cost_estimate=cost(0, MIB),
        name="sorted_targets",
    )(maps.reshape(count, 1, rows), earlier)


def coded_rows(value, out_ref):
    rows = value.shape[0]
    top = jnp.max(jnp.abs(value), axis=0, keepdims=True)
    exponent = jnp.floor(jnp.log2(jnp.maximum(top, 2.0**-108))) + 1.0
    code = jnp.floor(value * jnp.exp2(CODE_BITS - exponent) + 0.5).astype(jnp.int32)
    out_ref[:rows, :] = code.astype(jnp.int16)
    out_ref[rows:, :] = jnp.broadcast_to(exponent.astype(jnp.int32), (EXP_ROWS, CW)).astype(jnp.int16)


def update_body(count, pairs_ref, odd_ref, left_ref, projected_ref, *refs):
    contribs = refs[:count]
    out_refs = refs[-2 * count :]
    joint, width = left_ref.shape
    rows = joint // 2
    for start in range(0, count, 2):
        span = min(2, count - start)
        part = projected_ref[:, :, start * CW : (start + span) * CW].reshape(width, span * CW)
        product = jnp.dot(left_ref[...], part, preferred_element_type=jnp.float32)
        for step in range(start, start + span):
            reduced = contribs[step][0].astype(jnp.float32)
            reduced = reduced - product[:, (step - start) * CW : (step - start + 1) * CW]
            sides = swapped(odd_ref[0] > 0, *halves(reduced[:rows], reduced[rows:]))
            coded_rows(sides[0], out_refs[2 * step])
            coded_rows(sides[1], out_refs[2 * step + 1])


def update_group(odd, pairs, left, projected, place, contrib, earlier):
    joint, width = left.shape
    depth = projected.shape[0]
    count = pairs.shape[0]
    coded = (joint // 2 + EXP_ROWS, CW)

    def pick(step):
        return lambda i, pairs_ref, odd_ref: (pairs_ref[step], 0, 0)

    return pl.pallas_call(
        functools.partial(update_body, count),
        out_shape=[pltpu.HBM(coded, jnp.int16)] * (2 * count),
        grid_spec=pltpu.PrefetchScalarGridSpec(
            num_scalar_prefetch=2,
            grid=(1,),
            in_specs=[
                pl.BlockSpec((joint, width), lambda i, a, b: (0, 0)),
                pl.BlockSpec((depth, 2 * RK, count * CW), lambda i, a, b: (0, 0, place)),
            ]
            + [pl.BlockSpec((1, joint, CW), pick(step)) for step in range(count)]
            + untouched(len(earlier)),
            out_specs=[pl.BlockSpec(coded, lambda i, a, b: (0, 0))] * (2 * count),
        ),
        compiler_params=params(28),
        cost_estimate=cost(2 * joint * width * count * CW, 2 * count * CW * (width + 2 * joint)),
        name="update_group",
    )(pairs, odd, left, projected, *([contrib] * count), *earlier)


def scatter_body(count, has_partial, starts_ref, targets_ref, *refs):
    sources = refs[:count]
    partial_ref = refs[count] if has_partial else None
    out_ref, token_ref, values, one_hot = refs[-4:]
    joint = targets_ref.shape[1]
    rows = joint // 2

    @pl.when(pl.program_id(0) == 0)
    def _():
        for step in range(count):
            code = sources[step][:rows, :].astype(jnp.int32).astype(jnp.float32)
            exponent = sources[step][rows:, :].astype(jnp.int32).astype(jnp.float32)[:1]
            value = code * jnp.exp2(exponent - CODE_BITS)
            high = value.astype(jnp.bfloat16).astype(jnp.float32)
            low = value - high
            top, bottom = halves(high, low)
            values[step * joint : step * joint + rows, :] = top.astype(jnp.bfloat16)
            values[step * joint + rows : (step + 1) * joint, :] = bottom.astype(jnp.bfloat16)

    set_token(token_ref)
    lanes = lax.broadcasted_iota(jnp.int32, (WIN, rows), 1)
    batch = out_ref.shape[0]
    for place in range(batch):
        tile = pl.program_id(0) * batch + place
        lane = (lanes + tile * rows).astype(jnp.float32)
        parts = []
        for step in range(count):
            begin = jnp.minimum((starts_ref[step, tile] // 16) * 16, joint - WIN)
            begin = pl.multiple_of(begin, 16)
            target = targets_ref[step, pl.ds(begin, WIN), :]
            target = jnp.concatenate([target] * (rows // CW), axis=1)
            match = jnp.where(target == lane, 1.0, 0.0)
            one_hot[place, step * WIN : (step + 1) * WIN, :] = match.astype(jnp.bfloat16)
            parts.append(values[pl.ds(pl.multiple_of(step * joint + begin, 16), WIN), :])
        window = jnp.concatenate(parts, axis=0)
        total = lax.dot_general(
            window, one_hot[place], (((0,), (0,)), ((), ())), preferred_element_type=jnp.float32
        )
        total = total[:HALF] + total[HALF:]
        if has_partial:
            total = total + partial_ref[place]
        out_ref[place] = total.astype(out_ref.dtype)


def scatter_rows(starts, targets, coded, partial, out_dtype):
    count = len(coded)
    joint = targets.shape[1]
    rows = joint // 2
    tiles = starts.shape[1]
    batch = min(TILE_BATCH, tiles)
    has_partial = partial is not None
    tile_spec = pl.BlockSpec((batch, HALF, rows), lambda t: (t, 0, 0))
    whole = pl.BlockSpec((rows + EXP_ROWS, CW), lambda t: (0, 0))
    extra = [tile_spec] if has_partial else []
    operands = [partial] if has_partial else []
    return pl.pallas_call(
        functools.partial(scatter_body, count, has_partial),
        out_shape=[pltpu.HBM((tiles, HALF, rows), out_dtype), token_shape()],
        grid=(tiles // batch,),
        in_specs=[smem(), pl.BlockSpec(targets.shape, lambda t: (0, 0, 0))] + [whole] * count + extra,
        out_specs=[tile_spec, token_spec()],
        scratch_shapes=[
            pltpu.VMEM((count * joint, CW), jnp.bfloat16),
            pltpu.VMEM((batch, count * WIN, rows), jnp.bfloat16),
        ],
        compiler_params=params(36),
        cost_estimate=cost(2 * CW * count * WIN * rows * tiles, 8 * tiles * HALF * rows),
        name="scatter_rows",
    )(starts, targets, *coded, *operands)


def total_body(parts_ref, out_ref):
    sources, cols, rows = parts_ref.shape
    parts = parts_ref[...].astype(jnp.float32).reshape(sources // 2, 2, cols, rows)
    out_ref[...] = jnp.sum(parts, axis=0).reshape(2 * cols, rows).T


def total_rows(parts):
    sources, cols, rows = parts.shape
    return pl.pallas_call(
        total_body,
        out_shape=jax.ShapeDtypeStruct((rows, 2 * cols), jnp.float32),
        grid=(rows // CW,),
        in_specs=[pl.BlockSpec((sources, cols, CW), lambda i: (0, 0, i))],
        out_specs=pl.BlockSpec((CW, 2 * cols), lambda i: (i, 0)),
        compiler_params=params(6),
        cost_estimate=cost(sources * cols * rows, 2 * sources * cols * rows),
        name="total_rows",
    )(parts)


def per_device(
    rhs_pivot,
    block_pattern,
    diag_inverse,
    right_factor,
    left_factor,
    tile_ranks,
    contrib_rhs,
    parent_map,
):
    owner = lax.axis_index("owner")
    blk = lax.axis_index("blk")
    partners = lax.axis_size("blk")
    tiles = lax.axis_size("owner")
    ring = RING if tiles % RING == 0 else tiles
    inverse, right = diag_inverse[0], right_factor[0]
    rows = inverse.shape[0]
    groups = groups_of(partners // 2)
    all_pairs = jnp.bitwise_xor(blk // 2, jnp.array(sum(groups, []), jnp.int32))
    pairs = [jnp.bitwise_xor(blk // 2, jnp.array(group, jnp.int32)) for group in groups]
    batches = [
        [group[begin : begin + BATCH] for begin in range(0, len(group), BATCH)] for group in groups
    ]
    offsets = {
        tuple(batch): [2 * q + side for q in batch for side in range(2)]
        for group in batches
        for batch in group
    }
    fronts = [
        jnp.bitwise_xor(blk, jnp.array(sum((offsets[tuple(b)] for b in group), []), jnp.int32))
        for group in batches
    ]
    odd = (blk % 2).reshape(1)
    half = (owner % 2).reshape(1)
    second = ((owner + blk) % 2).reshape(1)

    def mate(tile, front):
        shift = front % 2
        place = (tile % ring + shift) ^ 1
        return tile // ring * ring + (place - shift) % ring

    across = [
        (tile * partners + front, mate(tile, front) * partners + front)
        for tile in range(tiles)
        for front in range(partners)
    ]

    def exchange(values, ks):
        steps = [[(i, i ^ k) for i in range(partners)] for k in ks]
        return [v if k == 0 else lax.ppermute(v, "blk", p) for v, k, p in zip(values, ks, steps)]

    def over_owner(value):
        return lax.all_to_all(value, "owner", split_axis=0, concat_axis=0, tiled=True)

    pattern = block_pattern.reshape(-1)
    masked, token = mask_all(rhs_pivot, pattern)
    front_rhs = lax.all_to_all(masked, "blk", split_axis=0, concat_axis=0, tiled=True)
    other_left = lax.ppermute(left_factor[0], ("owner", "blk"), across)
    kept, away = pack_contrib(half, contrib_rhs[0], token)
    got = lax.ppermute(away, ("owner", "blk"), across)

    ranks_here = lax.dynamic_index_in_dim(tile_ranks[0], owner, 1, keepdims=False)
    keep = jnp.arange(RK, dtype=jnp.int32)[None, :] < ranks_here[:, None]
    right_t = right_transposed(odd, right, keep.astype(jnp.float32).reshape(1, -1), ring)

    def tile_maps(tile):
        return lax.dynamic_slice_in_dim(parent_map, tile * rows, rows, 1)

    is_odd = (jnp.arange(partners) % 2 == 1)[:, None]
    other_maps = jnp.where(is_odd, tile_maps(mate(owner, 1)), tile_maps(mate(owner, 0)))
    maps = jnp.concatenate([tile_maps(owner), other_maps], axis=1)
    own_keys = lax.dynamic_index_in_dim(maps, blk, 0, keepdims=False).astype(jnp.float32)
    edges = (jnp.arange(tiles) * rows).astype(jnp.float32)
    ordered = jnp.sort(maps.astype(jnp.float32), axis=1)
    group_maps, starts = [], []
    for chosen in fronts:
        group_maps.append(jnp.take(ordered, chosen, axis=0))
        below = group_maps[-1][:, :, None] < edges[None, None, :]
        starts.append(jnp.sum(below.astype(jnp.int32), axis=1))

    solved, projected = [], []
    spread = [sorted_targets(keys, token) for keys in group_maps]
    ready = [later for _, later in spread] + [other_left, got]
    part, sent, _ = solve_group(pairs[0], odd, inverse, right_t, front_rhs, ring, ready)
    solved.append(part)
    projected.append(over_owner(sent))
    left, contrib, ready = sort_rows(second, own_keys, left_factor[0], other_left, kept, got)

    partial, token = None, None
    count = len(groups)
    for index in range(count):
        if index + 1 < count:
            part, sent, _ = solve_group(
                pairs[index + 1], odd, inverse, right_t, front_rhs, ring, [ready]
            )
            solved.append(part)
            projected.append(over_owner(sent))
        earlier = [] if partial is None else [token]
        arrived = []
        for place, batch in enumerate(batches[index]):
            chosen = jnp.bitwise_xor(blk // 2, jnp.array(batch, jnp.int32))
            coded = update_group(odd, chosen, left, projected[index], place, contrib, earlier)
            arrived += exchange(coded, offsets[tuple(batch)])
        dtype = jnp.float32 if index + 1 < count else jnp.bfloat16
        partial, token = scatter_rows(starts[index], spread[index][0], arrived, partial, dtype)
    parent_update = total_rows(over_owner(partial))
    pivot_solution = place_blocks(all_pairs, solved)
    return (pivot_solution, parent_update)


def solution(mesh):
    return jax.shard_map(
        per_device,
        mesh=mesh,
        in_specs=(
            P(None, "owner", "blk"),
            P(None, "owner", "blk"),
            P("blk", "owner", None),
            P("blk", "owner", None),
            P("blk", "owner", None),
            P("blk", None, None),
            P("blk", "owner", None),
            P(),
        ),
        out_specs=(P("blk", "owner", None), P("owner", "blk")),
        check_vma=False,
    )
```

```python
import functools

import jax
import jax.numpy as jnp
from jax import lax
from jax.experimental import pallas as pl
from jax.experimental.pallas import tpu as pltpu
from jax.sharding import PartitionSpec as P

RK = 64
CW = 128
WIN = 144
HALF = CW // 2
EXP_ROWS = 16
RING = 8
BATCH = 4
TILE_BATCH = 8
CODE_BITS = 14
MIB = 1024 * 1024


def vmem():
    return pl.BlockSpec(memory_space=pltpu.VMEM)


def smem():
    return pl.BlockSpec(memory_space=pltpu.SMEM)


def token_shape():
    return jax.ShapeDtypeStruct((8, CW), jnp.float32)


def token_spec():
    return pl.BlockSpec((8, CW), lambda *grid: (0, 0))


def set_token(token_ref):
    token_ref[...] = jnp.zeros_like(token_ref)


def untouched(count):
    return [pl.BlockSpec(memory_space=pltpu.HBM)] * count


def params(mib):
    return pltpu.CompilerParams(vmem_limit_bytes=mib * MIB)


def cost(flops, bytes_accessed):
    return pl.CostEstimate(flops=int(flops), bytes_accessed=int(bytes_accessed), transcendentals=0)


def groups_of(count):
    if count == 8:
        return [[4, 6, 2, 3], [5, 7, 1, 0]]
    return [list(range(count // 2, count)), list(range(count // 2))]


def halves(first, second):
    left = jnp.concatenate([first[:, :HALF], second[:, :HALF]], axis=1)
    right = jnp.concatenate([first[:, HALF:], second[:, HALF:]], axis=1)
    return left, right


def swapped(flag, first, second):
    return jnp.where(flag, second, first), jnp.where(flag, first, second)


def mask_body(pattern_ref, rhs_ref, out_ref, token_ref):
    for step in range(rhs_ref.shape[0]):
        front = pl.program_id(0) * rhs_ref.shape[0] + step
        keep = pattern_ref[front].astype(jnp.float32)
        out_ref[step] = (rhs_ref[step].astype(jnp.float32) * keep).astype(jnp.bfloat16)
    set_token(token_ref)


def mask_all(rhs, pattern):
    count, rows, cols = rhs.shape
    spec = pl.BlockSpec((4, rows, cols), lambda i: (i, 0, 0))
    return pl.pallas_call(
        mask_body,
        out_shape=[pltpu.HBM(rhs.shape, jnp.bfloat16), token_shape()],
        grid=(count // 4,),
        in_specs=[smem(), spec],
        out_specs=[spec, token_spec()],
        compiler_params=params(60),
        cost_estimate=cost(count * rows * cols, 4 * count * rows * cols),
        name="mask_all",
    )(pattern, rhs)


def right_body(ring, odd_ref, right_ref, keep_ref, out_ref):
    kept = (right_ref[...].astype(jnp.float32) * keep_ref[...]).T
    span = ring * RK
    pieces = []
    for begin in range(0, kept.shape[0], span):
        pieces += [kept[begin + RK : begin + span], kept[begin : begin + RK]]
    turned = jnp.concatenate(pieces, axis=0)
    out_ref[...] = jnp.where(odd_ref[0] > 0, turned, kept).astype(jnp.bfloat16)


def right_transposed(odd, right, keep, ring):
    rows, width = right.shape
    return pl.pallas_call(
        functools.partial(right_body, ring),
        out_shape=pltpu.HBM((width, rows), jnp.bfloat16),
        in_specs=[smem()] + [vmem()] * 2,
        out_specs=vmem(),
        compiler_params=params(16),
        cost_estimate=cost(rows * width, 4 * rows * width),
        name="right_transposed",
    )(odd, right, keep)


def solve_body(count, ring, pairs_ref, odd_ref, inverse_ref, right_ref, *refs):
    sources = refs[:count]
    solved_ref, projected_ref, token_ref = refs[-3:]
    set_token(token_ref)
    depth = projected_ref.shape[0]
    odd = odd_ref[0]
    for step in range(count):
        block = jnp.concatenate(halves(sources[step][0], sources[step][1]), axis=1)
        solved = jnp.dot(inverse_ref[...], block, preferred_element_type=jnp.float32)
        solved = solved.astype(jnp.bfloat16)
        solved_ref[step, 0], solved_ref[step, 1] = halves(solved[:, :CW], solved[:, CW:])
        projected = jnp.dot(right_ref[...], solved, preferred_element_type=jnp.float32)
        projected = projected.astype(jnp.bfloat16)
        span = slice(step * CW, (step + 1) * CW)
        for begin in range(0, depth, ring):
            for tile in range(0, ring, 2):
                row = (begin + tile) * RK
                pair = projected[row : row + 2 * RK]
                projected_ref[begin + tile + 1, :, span] = pair[:, CW:]
                projected_ref[begin + lax.rem(tile + 2 * odd, ring), :, span] = pair[:, :CW]


def solve_group(pairs, odd, inverse, right, blocks, ring, earlier):
    count = pairs.shape[0]
    rows = inverse.shape[0]
    width = right.shape[0]
    depth = width // RK

    def whole(shape):
        return pl.BlockSpec(shape, lambda i, pairs_ref, odd_ref: (0,) * len(shape))

    def pick(step):
        return lambda i, pairs_ref, odd_ref: (pairs_ref[step], 0, 0)

    return pl.pallas_call(
        functools.partial(solve_body, count, ring),
        out_shape=[
            pltpu.HBM((count, 2, rows, CW), jnp.bfloat16),
            pltpu.HBM((depth, 2 * RK, count * CW), jnp.bfloat16),
            token_shape(),
        ],
        grid_spec=pltpu.PrefetchScalarGridSpec(
            num_scalar_prefetch=2,
            grid=(1,),
            in_specs=[whole((rows, rows)), whole((width, rows))]
            + [pl.BlockSpec((2, rows, CW), pick(step)) for step in range(count)]
            + untouched(len(earlier)),
            out_specs=[
                whole((count, 2, rows, CW)),
                whole((depth, 2 * RK, count * CW)),
                token_spec(),
            ],
        ),
        compiler_params=params(60),
        cost_estimate=cost(4 * rows * (rows + width) * count * CW, 4 * count * CW * (2 * rows + width)),
        name="solve_group",
    )(pairs, odd, inverse, right, *([blocks] * count), *earlier)


def place_body(starts, pairs_ref, *refs):
    out_ref = refs[-1]
    step = pl.program_id(0)
    for begin, end, ref in zip(starts[:-1], starts[1:], refs[:-1]):

        @pl.when((step >= begin) & (step < end))
        def _(ref=ref):
            out_ref[0, :, :CW] = ref[0, 0]
            out_ref[0, :, CW:] = ref[0, 1]


def place_blocks(pairs, parts):
    starts = [0]
    for part in parts:
        starts.append(starts[-1] + part.shape[0])
    rows = parts[0].shape[2]

    def pick(begin, end):
        return lambda i, pairs_ref: (jnp.clip(i - begin, 0, end - begin - 1), 0, 0, 0)

    return pl.pallas_call(
        functools.partial(place_body, starts),
        out_shape=jax.ShapeDtypeStruct((1, rows, starts[-1] * 2 * CW), jnp.bfloat16),
        grid_spec=pltpu.PrefetchScalarGridSpec(
            num_scalar_prefetch=1,
            grid=(starts[-1],),
            in_specs=[
                pl.BlockSpec((1, 2, rows, CW), pick(begin, end))
                for begin, end in zip(starts[:-1], starts[1:])
            ],
            out_specs=pl.BlockSpec((1, rows, 2 * CW), lambda i, pairs_ref: (0, 0, pairs_ref[i])),
        ),
        compiler_params=params(6),
        cost_estimate=cost(0, 8 * rows * starts[-1] * CW),
        name="place_blocks",
    )(pairs, *parts)


def pack_body(high_ref, contrib_ref, after_ref, keep_ref, send_ref):
    high = high_ref[0] > 0
    for step in range(keep_ref.shape[1] // CW):
        even = contrib_ref[:, 2 * step * CW : (2 * step + 1) * CW]
        other = contrib_ref[:, (2 * step + 1) * CW : (2 * step + 2) * CW]
        span = slice(step * CW, (step + 1) * CW)
        keep_ref[:, span], send_ref[:, span] = swapped(high, *halves(even, other))


def pack_contrib(high, contrib, earlier):
    rows, cols = contrib.shape
    spec = pl.BlockSpec((rows, cols // 4), lambda i: (0, i))
    return pl.pallas_call(
        pack_body,
        out_shape=[pltpu.HBM((rows, cols // 2), jnp.bfloat16)] * 2,
        grid=(2,),
        in_specs=[smem(), pl.BlockSpec((rows, cols // 2), lambda i: (0, i))] + untouched(1),
        out_specs=[spec] * 2,
        compiler_params=params(60),
        cost_estimate=cost(0, MIB),
        name="pack_contrib",
    )(high, contrib, earlier)


def ordering(keys):
    rows = keys.shape[1]
    column = jnp.broadcast_to(keys, (CW, rows)).T
    smaller = (jnp.concatenate([column] * (rows // CW), axis=1) < keys).astype(jnp.float32)
    rank = jnp.sum(smaller, axis=0, keepdims=True)
    place = lax.broadcasted_iota(jnp.int32, (rows, rows), 0).astype(jnp.float32)
    return jnp.where(place == rank, 1.0, 0.0).astype(jnp.bfloat16)


def sort_body(
    high_ref, keys_ref, own_ref, other_ref, kept_ref, got_ref, left_out, contrib_out, token_ref, one_hot
):
    rows = own_ref.shape[0]

    @pl.when(pl.program_id(0) == 0)
    def _():
        one_hot[...] = ordering(keys_ref[...])
        set_token(token_ref)

    def sort(value, begin):
        order = one_hot[:, begin : begin + rows]
        return jnp.dot(order, value, preferred_element_type=jnp.float32)

    own, other = sort(own_ref[...], 0), sort(other_ref[...], rows)
    low, top = swapped(high_ref[0] > 0, own, other)
    for step in range(low.shape[1] // CW):
        span = slice(step * CW, (step + 1) * CW)
        pair = halves(low[:, span], top[:, span])
        left_out[:, 2 * step * CW : (2 * step + 1) * CW] = pair[0].astype(jnp.bfloat16)
        left_out[:, (2 * step + 1) * CW : (2 * step + 2) * CW] = pair[1].astype(jnp.bfloat16)

    contrib = sort(kept_ref[...], 0) + sort(got_ref[...], rows)
    for step in range(contrib_out.shape[0]):
        contrib_out[step] = contrib[:, step * CW : (step + 1) * CW].astype(jnp.bfloat16)


def sort_rows(high, keys, own, other, kept, got):
    rows, width = own.shape
    cols = kept.shape[1]
    joint = 2 * rows
    steps = min(4, cols // CW)
    spread = min(steps, width // CW)
    return pl.pallas_call(
        sort_body,
        out_shape=[
            pltpu.HBM((joint, 2 * width), jnp.bfloat16),
            pltpu.HBM((cols // CW, joint, CW), jnp.bfloat16),
            token_shape(),
        ],
        grid=(steps,),
        in_specs=[
            smem(),
            pl.BlockSpec((1, joint), lambda i: (0, 0)),
            pl.BlockSpec((rows, width // spread), lambda i: (0, i % spread)),
            pl.BlockSpec((rows, width // spread), lambda i: (0, i % spread)),
            pl.BlockSpec((rows, cols // steps), lambda i: (0, i)),
            pl.BlockSpec((rows, cols // steps), lambda i: (0, i)),
        ],
        out_specs=[
            pl.BlockSpec((joint, 2 * width // spread), lambda i: (0, i % spread)),
            pl.BlockSpec((cols // CW // steps, joint, CW), lambda i: (i, 0, 0)),
            token_spec(),
        ],
        scratch_shapes=[pltpu.VMEM((joint, joint), jnp.bfloat16)],
        compiler_params=params(28),
        cost_estimate=cost(2 * joint * rows * (2 * width + 2 * cols), 8 * rows * (width + cols)),
        name="sort_rows",
    )(high, keys.reshape(1, joint), own, other, kept, got)


def target_body(keys_ref, after_ref, out_ref, token_ref):
    for step in range(keys_ref.shape[0]):
        keys = keys_ref[step]
        out_ref[step] = jnp.broadcast_to(keys, (CW, keys.shape[1])).T
    set_token(token_ref)


def sorted_targets(maps, earlier):
    count, rows = maps.shape
    batch = 2 if count % 2 == 0 else 1
    return pl.pallas_call(
        target_body,
        out_shape=[pltpu.HBM((count, rows, CW), jnp.float32), token_shape()],
        grid=(count // batch,),
        in_specs=[pl.BlockSpec((batch, 1, rows), lambda i: (i, 0, 0))] + untouched(1),
        out_specs=[pl.BlockSpec((batch, rows, CW), lambda i: (i, 0, 0)), token_spec()],
        compiler_params=params(16),
        cost_estimate=cost(0, MIB),
        name="sorted_targets",
    )(maps.reshape(count, 1, rows), earlier)


def coded_rows(value, out_ref):
    rows = value.shape[0]
    top = jnp.max(jnp.abs(value), axis=0, keepdims=True)
    exponent = jnp.floor(jnp.log2(jnp.maximum(top, 2.0**-108))) + 1.0
    code = jnp.floor(value * jnp.exp2(CODE_BITS - exponent) + 0.5).astype(jnp.int32)
    out_ref[:rows, :] = code.astype(jnp.int16)
    out_ref[rows:, :] = jnp.broadcast_to(exponent.astype(jnp.int32), (EXP_ROWS, CW)).astype(jnp.int16)


def update_body(count, pairs_ref, odd_ref, left_ref, projected_ref, *refs):
    contribs = refs[:count]
    out_refs = refs[-2 * count :]
    joint, width = left_ref.shape
    rows = joint // 2
    for start in range(0, count, 2):
        span = min(2, count - start)
        part = projected_ref[:, :, start * CW : (start + span) * CW].reshape(width, span * CW)
        product = jnp.dot(left_ref[...], part, preferred_element_type=jnp.float32)
        for step in range(start, start + span):
            reduced = contribs[step][0].astype(jnp.float32)
            reduced = reduced - product[:, (step - start) * CW : (step - start + 1) * CW]
            sides = swapped(odd_ref[0] > 0, *halves(reduced[:rows], reduced[rows:]))
            coded_rows(sides[0], out_refs[2 * step])
            coded_rows(sides[1], out_refs[2 * step + 1])


def update_group(odd, pairs, left, projected, place, contrib, earlier):
    joint, width = left.shape
    depth = projected.shape[0]
    count = pairs.shape[0]
    coded = (joint // 2 + EXP_ROWS, CW)

    def pick(step):
        return lambda i, pairs_ref, odd_ref: (pairs_ref[step], 0, 0)

    return pl.pallas_call(
        functools.partial(update_body, count),
        out_shape=[pltpu.HBM(coded, jnp.int16)] * (2 * count),
        grid_spec=pltpu.PrefetchScalarGridSpec(
            num_scalar_prefetch=2,
            grid=(1,),
            in_specs=[
                pl.BlockSpec((joint, width), lambda i, a, b: (0, 0)),
                pl.BlockSpec((depth, 2 * RK, count * CW), lambda i, a, b: (0, 0, place)),
            ]
            + [pl.BlockSpec((1, joint, CW), pick(step)) for step in range(count)]
            + untouched(len(earlier)),
            out_specs=[pl.BlockSpec(coded, lambda i, a, b: (0, 0))] * (2 * count),
        ),
        compiler_params=params(60),
        cost_estimate=cost(2 * joint * width * count * CW, 2 * count * CW * (width + 2 * joint)),
        name="update_group",
    )(pairs, odd, left, projected, *([contrib] * count), *earlier)


def scatter_body(count, has_partial, starts_ref, targets_ref, *refs):
    sources = refs[:count]
    partial_ref = refs[count] if has_partial else None
    out_ref, token_ref, values, one_hot = refs[-4:]
    joint = targets_ref.shape[1]
    rows = joint // 2

    @pl.when(pl.program_id(0) == 0)
    def _():
        for step in range(count):
            code = sources[step][:rows, :].astype(jnp.int32).astype(jnp.float32)
            exponent = sources[step][rows:, :].astype(jnp.int32).astype(jnp.float32)[:1]
            value = code * jnp.exp2(exponent - CODE_BITS)
            high = value.astype(jnp.bfloat16).astype(jnp.float32)
            low = value - high
            top, bottom = halves(high, low)
            values[step * joint : step * joint + rows, :] = top.astype(jnp.bfloat16)
            values[step * joint + rows : (step + 1) * joint, :] = bottom.astype(jnp.bfloat16)

    set_token(token_ref)
    lanes = lax.broadcasted_iota(jnp.int32, (WIN, rows), 1)
    batch = out_ref.shape[0]
    for place in range(batch):
        tile = pl.program_id(0) * batch + place
        lane = (lanes + tile * rows).astype(jnp.float32)
        parts = []
        for step in range(count):
            begin = jnp.minimum((starts_ref[step, tile] // 16) * 16, joint - WIN)
            begin = pl.multiple_of(begin, 16)
            target = targets_ref[step, pl.ds(begin, WIN), :]
            target = jnp.concatenate([target] * (rows // CW), axis=1)
            match = jnp.where(target == lane, 1.0, 0.0)
            one_hot[place, step * WIN : (step + 1) * WIN, :] = match.astype(jnp.bfloat16)
            parts.append(values[pl.ds(pl.multiple_of(step * joint + begin, 16), WIN), :])
        window = jnp.concatenate(parts, axis=0)
        total = lax.dot_general(
            window, one_hot[place], (((0,), (0,)), ((), ())), preferred_element_type=jnp.float32
        )
        total = total[:HALF] + total[HALF:]
        if has_partial:
            total = total + partial_ref[place]
        out_ref[place] = total.astype(out_ref.dtype)


def scatter_rows(starts, targets, coded, partial, out_dtype):
    count = len(coded)
    joint = targets.shape[1]
    rows = joint // 2
    tiles = starts.shape[1]
    batch = min(TILE_BATCH, tiles)
    has_partial = partial is not None
    tile_spec = pl.BlockSpec((batch, HALF, rows), lambda t: (t, 0, 0))
    whole = pl.BlockSpec((rows + EXP_ROWS, CW), lambda t: (0, 0))
    extra = [tile_spec] if has_partial else []
    operands = [partial] if has_partial else []
    return pl.pallas_call(
        functools.partial(scatter_body, count, has_partial),
        out_shape=[pltpu.HBM((tiles, HALF, rows), out_dtype), token_shape()],
        grid=(tiles // batch,),
        in_specs=[smem(), pl.BlockSpec(targets.shape, lambda t: (0, 0, 0))] + [whole] * count + extra,
        out_specs=[tile_spec, token_spec()],
        scratch_shapes=[
            pltpu.VMEM((count * joint, CW), jnp.bfloat16),
            pltpu.VMEM((batch, count * WIN, rows), jnp.bfloat16),
        ],
        compiler_params=params(36),
        cost_estimate=cost(2 * CW * count * WIN * rows * tiles, 8 * tiles * HALF * rows),
        name="scatter_rows",
    )(starts, targets, *coded, *operands)


def total_body(parts_ref, out_ref):
    sources, cols, rows = parts_ref.shape
    parts = parts_ref[...].astype(jnp.float32).reshape(sources // 2, 2, cols, rows)
    out_ref[...] = jnp.sum(parts, axis=0).reshape(2 * cols, rows).T


def total_rows(parts):
    sources, cols, rows = parts.shape
    return pl.pallas_call(
        total_body,
        out_shape=jax.ShapeDtypeStruct((rows, 2 * cols), jnp.float32),
        grid=(rows // CW,),
        in_specs=[pl.BlockSpec((sources, cols, CW), lambda i: (0, 0, i))],
        out_specs=pl.BlockSpec((CW, 2 * cols), lambda i: (i, 0)),
        compiler_params=params(6),
        cost_estimate=cost(sources * cols * rows, 2 * sources * cols * rows),
        name="total_rows",
    )(parts)


def per_device(
    rhs_pivot,
    block_pattern,
    diag_inverse,
    right_factor,
    left_factor,
    tile_ranks,
    contrib_rhs,
    parent_map,
):
    owner = lax.axis_index("owner")
    blk = lax.axis_index("blk")
    partners = lax.axis_size("blk")
    tiles = lax.axis_size("owner")
    ring = RING if tiles % RING == 0 else tiles
    inverse, right = diag_inverse[0], right_factor[0]
    rows = inverse.shape[0]
    groups = groups_of(partners // 2)
    all_pairs = jnp.bitwise_xor(blk // 2, jnp.array(sum(groups, []), jnp.int32))
    pairs = [jnp.bitwise_xor(blk // 2, jnp.array(group, jnp.int32)) for group in groups]
    batches = [
        [group[begin : begin + BATCH] for begin in range(0, len(group), BATCH)] for group in groups
    ]
    offsets = {
        tuple(batch): [2 * q + side for q in batch for side in range(2)]
        for group in batches
        for batch in group
    }
    fronts = [
        jnp.bitwise_xor(blk, jnp.array(sum((offsets[tuple(b)] for b in group), []), jnp.int32))
        for group in batches
    ]
    odd = (blk % 2).reshape(1)
    half = (owner % 2).reshape(1)
    second = ((owner + blk) % 2).reshape(1)

    def mate(tile, front):
        shift = front % 2
        place = (tile % ring + shift) ^ 1
        return tile // ring * ring + (place - shift) % ring

    across = [
        (tile * partners + front, mate(tile, front) * partners + front)
        for tile in range(tiles)
        for front in range(partners)
    ]

    def exchange(values, ks):
        steps = [[(i, i ^ k) for i in range(partners)] for k in ks]
        return [v if k == 0 else lax.ppermute(v, "blk", p) for v, k, p in zip(values, ks, steps)]

    def over_owner(value):
        return lax.all_to_all(value, "owner", split_axis=0, concat_axis=0, tiled=True)

    pattern = block_pattern.reshape(-1)
    masked, token = mask_all(rhs_pivot, pattern)
    front_rhs = lax.all_to_all(masked, "blk", split_axis=0, concat_axis=0, tiled=True)
    other_left = lax.ppermute(left_factor[0], ("owner", "blk"), across)
    kept, away = pack_contrib(half, contrib_rhs[0], token)
    got = lax.ppermute(away, ("owner", "blk"), across)

    ranks_here = lax.dynamic_index_in_dim(tile_ranks[0], owner, 1, keepdims=False)
    keep = jnp.arange(RK, dtype=jnp.int32)[None, :] < ranks_here[:, None]
    right_t = right_transposed(odd, right, keep.astype(jnp.float32).reshape(1, -1), ring)

    def tile_maps(tile):
        return lax.dynamic_slice_in_dim(parent_map, tile * rows, rows, 1)

    is_odd = (jnp.arange(partners) % 2 == 1)[:, None]
    other_maps = jnp.where(is_odd, tile_maps(mate(owner, 1)), tile_maps(mate(owner, 0)))
    maps = jnp.concatenate([tile_maps(owner), other_maps], axis=1)
    own_keys = lax.dynamic_index_in_dim(maps, blk, 0, keepdims=False).astype(jnp.float32)
    edges = (jnp.arange(tiles) * rows).astype(jnp.float32)
    ordered = jnp.sort(maps.astype(jnp.float32), axis=1)
    group_maps, starts = [], []
    for chosen in fronts:
        group_maps.append(jnp.take(ordered, chosen, axis=0))
        below = group_maps[-1][:, :, None] < edges[None, None, :]
        starts.append(jnp.sum(below.astype(jnp.int32), axis=1))

    solved, projected = [], []
    spread = [sorted_targets(keys, token) for keys in group_maps]
    ready = [later for _, later in spread] + [other_left, got]
    part, sent, _ = solve_group(pairs[0], odd, inverse, right_t, front_rhs, ring, ready)
    solved.append(part)
    projected.append(over_owner(sent))
    left, contrib, ready = sort_rows(second, own_keys, left_factor[0], other_left, kept, got)

    partial, token = None, None
    count = len(groups)
    for index in range(count):
        if index + 1 < count:
            part, sent, _ = solve_group(
                pairs[index + 1], odd, inverse, right_t, front_rhs, ring, [ready]
            )
            solved.append(part)
            projected.append(over_owner(sent))
        earlier = [] if partial is None else [token]
        arrived = []
        for place, batch in enumerate(batches[index]):
            chosen = jnp.bitwise_xor(blk // 2, jnp.array(batch, jnp.int32))
            coded = update_group(odd, chosen, left, projected[index], place, contrib, earlier)
            arrived += exchange(coded, offsets[tuple(batch)])
        dtype = jnp.float32 if index + 1 < count else jnp.bfloat16
        partial, token = scatter_rows(starts[index], spread[index][0], arrived, partial, dtype)
    parent_update = total_rows(over_owner(partial))
    pivot_solution = place_blocks(all_pairs, solved)
    return (pivot_solution, parent_update)


def solution(mesh):
    return jax.shard_map(
        per_device,
        mesh=mesh,
        in_specs=(
            P(None, "owner", "blk"),
            P(None, "owner", "blk"),
            P("blk", "owner", None),
            P("blk", "owner", None),
            P("blk", "owner", None),
            P("blk", None, None),
            P("blk", "owner", None),
            P(),
        ),
        out_specs=(P("blk", "owner", None), P("owner", "blk")),
        check_vma=False,
    )
```
